128 devices in a mesh: owner: 64 (over y, x, z), split: 2 (over core).
Axes of the slice: x: 4, y: 4, z: 4, core: 2. Of those that a mesh axis runs over, the one named last changes fastest.
Arguments:
- embeddings: bfloat16 [65536, 1024], P(('owner', 'split')), may hold values from -6 to 6
- cluster: int32 [65536, 1], P(('owner', 'split')), may hold values from 0 to 63; in each aligned block of 512 rows (0 to 511, 512 to 1023, ...) at most 32 rows name the same one
- order: int32 [65536], P(('owner', 'split')), may hold values from 0 to 65535, each once
Outputs:
- best: float32 [65536], P(('owner', 'split'))
The draws below stay inside these ranges and needn't reach their ends.
Inputs may be any that keep to these rules, and one draw needn't show every extreme that they name: Among the 512 rows of one device (aligned blocks of rows) no cluster id appears more than 32 times, and in some blocks one appears exactly 32 times; every cluster has rows. `order`: each number appears once.
All inputs are finite; a program needn't handle non-finite values.
Results may differ from the reference program's by a relative error of at most 0.0014.
Values may be sent and summed in bfloat16 or wider, within the bound.
No kernel may reach another device: no remote copies, remote signals or barrier semaphores. Data moves between devices by JAX's collectives and lax.ppermute only.
A program may use at most 64 MiB of HBM per device.

```python
import math
import jax
import jax.numpy as jnp
import numpy as np
from jax import lax

D = 1024
ROWS_DEV = 512
NCLUST = 64
CAP = 32
ROWS = 65536
DEVICES = 128


def steps_of(own_key, dims, split, least, high):
    level = 1.0
    for dim, blocks in split:
        steps = jax.random.uniform(jax.random.fold_in(jax.random.fold_in(own_key, 6), dim), (blocks,), jnp.float32, least / len(split), high / len(split))
        level = level * jnp.repeat(jnp.exp(steps), dims[dim] // blocks).reshape((-1,) + (1,) * (len(dims) - 1 - dim))
    return level


def deal_out(own_key, own, number, rows, amount, top, most, slope):
    ranking = jax.random.permutation(own_key, amount)
    packed, common = portions_of(amount, rows * top, most, slope, True), portions_of(amount, rows * top, most, slope, False)
    places = jnp.arange(amount)

    def named(tallies, rotation):
        used = int((tallies > 0).sum())
        fixed = max(1, used // 4)
        moved = fixed + (places - fixed + rotation * (used - fixed)) % max(1, amount - fixed)
        return jnp.zeros((amount,), jnp.int32).at[ranking[jnp.where(places < fixed, places, moved)]].set(jnp.asarray(tallies, jnp.int32))

    tallies = jnp.where(number % 4 == 0, named(packed, number // 4), named(common, number - number // 4 - 1))
    mixed = jax.random.permutation(jax.random.fold_in(own, 3), amount)
    donor, sink = mixed[0:amount // 2 * 2:2], mixed[1:amount // 2 * 2:2]
    margin = jnp.minimum(tallies[donor] - 1, most - tallies[sink]) // 2
    margin = jnp.where((donor == ranking[0]) | (sink == ranking[0]) | (tallies[sink] == 0), 0, jnp.maximum(margin, 0))
    moved = jax.random.randint(jax.random.fold_in(own, 4), (amount // 2,), 0, 1 << 20) % (margin + 1)
    tallies = tallies.at[donor].add(-moved).at[sink].add(moved)
    labels = jnp.searchsorted(jnp.cumsum(tallies), jnp.arange(rows * top), side="right").astype(jnp.int32)
    table = labels.reshape(top, rows).T
    table = table[jax.random.permutation(jax.random.fold_in(own, 1), rows)]
    rotation = jax.random.randint(jax.random.fold_in(own, 2), (rows, 1), 0, top)
    return jnp.take_along_axis(table, (jnp.arange(top)[None, :] + rotation) % top, axis=1)


def portions_of(number_of, total, most, lean, full):
    weights = [(1 << 20) // math.isqrt(standing ** lean) + 1 for standing in range(1, number_of + 1)]
    largest = most if full else min(most, max(-(-total // number_of), total * weights[0] // sum(weights)))
    least = 1 if total - largest >= number_of - 1 else 0
    holding, spare = [largest] + [least] * (number_of - 1), total - largest - least * (number_of - 1)
    while spare > 0:
        free = [i for i in range(1, number_of) if holding[i] < largest] or [i for i in range(1, number_of) if holding[i] < most]
        mass, remaining = sum([weights[i] for i in free]), spare
        for i in free:
            more = min(most - holding[i], max(1, remaining * weights[i] // mass), spare)
            holding[i] = holding[i] + more
            spare = spare - more
    return np.array(holding)


def normal_values(rng, dims, width, most, pieces=(), kind=jnp.bfloat16):
    entries = jax.random.normal(rng, dims, jnp.float32) * width
    if len(pieces) > 0:
        entries = steps_of(rng, dims, pieces, -0.22, 0.18) * entries
    return jnp.clip(entries, min=-most, max=most).astype(kind)


def setup_inputs(seed: int = 0) -> dict:
    splits = jax.random.split(jax.random.key(seed), 4)
    embeddings = normal_values(splits[0], (ROWS, D), 1.0, 6.0, ((0, 128),))
    cluster_keys = jax.random.split(jax.random.fold_in(splits[1], 1), ROWS // ROWS_DEV)
    cluster_turns = jax.random.permutation(jax.random.fold_in(splits[1], 3), ROWS // ROWS_DEV)
    cluster = jax.vmap(lambda own, number: deal_out(jax.random.fold_in(splits[1], 2), own, number, ROWS_DEV, NCLUST, 1, CAP, 2))(cluster_keys, cluster_turns).reshape((ROWS, 1))
    order = jax.random.permutation(splits[2], ROWS).astype(jnp.int32)
    return {"embeddings": embeddings, "cluster": cluster, "order": order}


query_block = 512

def reference(embeddings, cluster, order):
    e = embeddings.astype(jnp.float32)
    unit = (e * lax.rsqrt(lax.optimization_barrier(jnp.sum(e * e, axis=1, keepdims=True)) + 1e-06)).astype(jnp.bfloat16)
    cid = cluster[:, 0]
    sort_key = cid * ROWS + order
    perm = jnp.argsort(sort_key).astype(jnp.int32)
    sorted_unit = unit[perm]
    sorted_cid = cid[perm]
    sorted_order = order[perm]
    reach = DEVICES * CAP
    padded_unit = jnp.concatenate([jnp.zeros((reach, D), jnp.bfloat16), sorted_unit], axis=0)
    padded_cid = jnp.concatenate([jnp.full((reach,), -1, jnp.int32), sorted_cid.astype(jnp.int32)], axis=0)
    padded_order = jnp.concatenate([jnp.full((reach,), ROWS, jnp.int32), sorted_order.astype(jnp.int32)], axis=0)

    def one_block(index):
        start = (index * query_block).astype(jnp.int32)
        queries = lax.dynamic_slice_in_dim(sorted_unit, start, query_block, 0)
        q_cid = lax.dynamic_slice_in_dim(sorted_cid, start, query_block, 0)
        q_order = lax.dynamic_slice_in_dim(sorted_order, start, query_block, 0)
        keys = lax.dynamic_slice_in_dim(padded_unit, start, reach + query_block, 0)
        k_cid = lax.dynamic_slice_in_dim(padded_cid, start, reach + query_block, 0)
        k_order = lax.dynamic_slice_in_dim(padded_order, start, reach + query_block, 0)
        sims = jnp.dot(queries.astype(jnp.float32), keys.astype(jnp.float32).T)
        valid = (k_cid[None, :] == q_cid[:, None]) & (k_order[None, :] < q_order[:, None])
        return lax.optimization_barrier(jnp.max(jnp.where(valid, sims, jnp.float32(-1.0)), axis=1))
    blocks = lax.map(one_block, jnp.arange(ROWS // query_block, dtype=jnp.int32))
    return jnp.zeros((ROWS,), jnp.float32).at[perm].set(blocks.reshape(ROWS))
```

```python
import functools
import jax
import jax.numpy as jnp
from jax import lax
from jax.experimental import pallas as pl
from jax.experimental.pallas import tpu as pltpu
from jax.sharding import PartitionSpec as P

CAP = 32
LANES = 128
EMPTY = 262144.0
TILE = 512


def pack_kernel(emb_ref, cid_ref, order_ref, out_ref, target_ref, unit_ref):
    step = pl.program_id(0)
    rows, width = emb_ref.shape

    @pl.when(step == 0)
    def _():
        chunk = 128
        for r in range(rows // chunk):
            part = pl.ds(r * chunk, chunk)
            e = emb_ref[part, :].astype(jnp.float32)
            scale = lax.rsqrt(jnp.sum(e * e, axis=1, keepdims=True) + 1e-06)
            unit_ref[part, :width] = (e * scale).astype(jnp.bfloat16)
        cid = cid_ref[...].astype(jnp.float32)
        column = jnp.transpose(jnp.broadcast_to(cid, (LANES, rows)))
        above = lax.broadcasted_iota(jnp.int32, (rows, LANES), 0)
        for j in range(rows // LANES):
            lanes = slice(j * LANES, (j + 1) * LANES)
            here = lax.broadcasted_iota(jnp.int32, (rows, LANES), 1) + j * LANES
            same = (column == cid[:, lanes]) & (above < here)
            place = jnp.sum(same.astype(jnp.float32), axis=0, keepdims=True)
            target_ref[:, lanes] = (cid[:, lanes] * CAP + place).astype(jnp.int32)
        code = order_ref[...] + 1
        high = jnp.broadcast_to((code >> 8).astype(jnp.float32), (LANES // 2, rows))
        low = jnp.broadcast_to((code & 255).astype(jnp.float32), (LANES // 2, rows))
        both = jnp.concatenate([high, low], axis=0)
        unit_ref[:, width:] = jnp.transpose(both).astype(jnp.bfloat16)

    group, cap, full = out_ref.shape
    slots = group * cap
    slot = lax.broadcasted_iota(jnp.int32, (slots, rows), 0) + step * slots
    place = (slot == target_ref[...]).astype(jnp.float32).astype(jnp.bfloat16)
    packed = jnp.dot(place, unit_ref[...], preferred_element_type=jnp.float32)
    out_ref[...] = packed.astype(jnp.bfloat16).reshape(group, cap, full)


def pack(embeddings, cid, order, owners):
    rows, width = embeddings.shape
    full = width + LANES
    group = TILE // CAP
    return pl.pallas_call(
        pack_kernel,
        grid=(owners // group,),
        out_shape=(
            jax.ShapeDtypeStruct((owners, CAP, full), jnp.bfloat16),
            jax.ShapeDtypeStruct((1, rows), jnp.int32),
        ),
        in_specs=[
            pl.BlockSpec((rows, width), lambda i: (0, 0)),
            pl.BlockSpec((1, rows), lambda i: (0, 0)),
            pl.BlockSpec((1, rows), lambda i: (0, 0)),
        ],
        out_specs=(
            pl.BlockSpec((group, CAP, full), lambda i: (i, 0, 0)),
            pl.BlockSpec((1, rows), lambda i: (0, 0)),
        ),
        scratch_shapes=[pltpu.VMEM((rows, full), jnp.bfloat16)],
        compiler_params=pltpu.CompilerParams(vmem_limit_bytes=32 * 2**20),
        name="pack_rows",
    )(embeddings, cid, order)


def read_ranks(x_ref, width, column_ref, row_ref):
    count = x_ref.shape[0]
    for t in range(count // TILE):
        part = slice(t * TILE, (t + 1) * TILE)
        two = x_ref[part, width:].astype(jnp.float32)
        other = pltpu.roll(two, LANES // 2, 1)
        lane = lax.broadcasted_iota(jnp.int32, two.shape, 1)
        code = jnp.where(lane < LANES // 2, two * 256.0 + other, two + other * 256.0)
        code = jnp.where(code == 0.0, EMPTY, code)
        if column_ref is not None:
            column_ref[part, :] = code
        if row_ref is not None:
            row_ref[:, part] = jnp.transpose(code)[:8, :]


def compare(x, y, column, row, rows_best, columns_best):
    sims = lax.dot_general(x, y, (((1,), (1,)), ((), ())), preferred_element_type=jnp.float32)
    columns = []
    for j in range(sims.shape[1] // LANES):
        lanes = slice(j * LANES, (j + 1) * LANES)
        s = sims[:, lanes]
        earlier = row[:1, lanes] < column
        rows_best = jnp.maximum(rows_best, jnp.where(earlier, s, -1.0))
        if columns_best is not None:
            later = jnp.where(earlier, -1.0, s)
            columns.append(jnp.max(later.reshape(-1, 8, LANES), axis=0))
    if columns_best is None:
        return rows_best, None
    return rows_best, jnp.maximum(columns_best, jnp.concatenate(columns, axis=1))


def own_kernel(width, x_ref, out_ref, column_ref, row_ref, rows_ref, columns_ref):
    count = x_ref.shape[0]
    read_ranks(x_ref, width, column_ref, row_ref)
    rows_ref[...] = jnp.full(rows_ref.shape, -1.0, jnp.float32)
    columns_ref[...] = jnp.full(columns_ref.shape, -1.0, jnp.float32)
    tiles = count // TILE
    for i in range(tiles):
        a = slice(i * TILE, (i + 1) * TILE)
        for j in range(i, tiles):
            b = slice(j * TILE, (j + 1) * TILE)
            best, across = compare(
                x_ref[a, :width], x_ref[b, :width], column_ref[a, :], row_ref[:, b],
                rows_ref[a, :], columns_ref[:, b] if j > i else None,
            )
            rows_ref[a, :] = best
            if across is not None:
                columns_ref[:, b] = across
    for i in range(tiles):
        a = slice(i * TILE, (i + 1) * TILE)
        best = jnp.max(jnp.transpose(rows_ref[a, :]), axis=0, keepdims=True)
        best = jnp.maximum(best, jnp.max(columns_ref[:, a], axis=0, keepdims=True))
        out_ref[:, a] = jnp.broadcast_to(best, (8, TILE))


def own_pairs(x, width):
    count, full = x.shape
    pairs = count * (count + TILE) // 2
    return pl.pallas_call(
        functools.partial(own_kernel, width),
        out_shape=jax.ShapeDtypeStruct((8, count), jnp.float32),
        in_specs=[pl.BlockSpec(memory_space=pltpu.VMEM)],
        out_specs=pl.BlockSpec(memory_space=pltpu.VMEM),
        scratch_shapes=[
            pltpu.VMEM((count, LANES), jnp.float32),
            pltpu.VMEM((8, count), jnp.float32),
            pltpu.VMEM((count, LANES), jnp.float32),
            pltpu.VMEM((8, count), jnp.float32),
        ],
        compiler_params=pltpu.CompilerParams(vmem_limit_bytes=40 * 2**20),
        cost_estimate=pl.CostEstimate(
            flops=2 * pairs * width, bytes_accessed=2 * count * full, transcendentals=0
        ),
        name="own_pairs",
    )(x)


def cross_kernel(width, core_ref, x_ref, y_ref, own_ref, out_ref, column_ref, row_ref, rows_ref, columns_ref):
    count = x_ref.shape[0]
    core = core_ref[0]
    read_ranks(x_ref, width, column_ref, None)
    read_ranks(y_ref, width, None, row_ref)
    rows_ref[...] = jnp.full(rows_ref.shape, -1.0, jnp.float32)
    columns_ref[...] = jnp.full(columns_ref.shape, -1.0, jnp.float32)
    tiles = count // TILE
    half = tiles // 2
    for t in range(tiles * half):
        i = jnp.where(core == 0, t // half, half + t % half)
        j = jnp.where(core == 0, t % half, t // half)
        a = pl.ds(pl.multiple_of(i * TILE, TILE), TILE)
        b = pl.ds(pl.multiple_of(j * TILE, TILE), TILE)
        best, across = compare(
            x_ref[a, :width], y_ref[b, :width], column_ref[a, :], row_ref[:, b],
            rows_ref[a, :], columns_ref[:, b],
        )
        rows_ref[a, :] = best
        columns_ref[:, b] = across
    parity = lax.broadcasted_iota(jnp.int32, (8, LANES), 0) % 2
    for g in range(count // LANES):
        a = slice(g * LANES, (g + 1) * LANES)
        mine = jnp.max(jnp.transpose(rows_ref[a, :]), axis=0, keepdims=True)
        mine = jnp.maximum(mine, own_ref[:1, a])
        theirs = jnp.max(columns_ref[:, a], axis=0, keepdims=True)
        out_ref[g * 8 : (g + 1) * 8, :] = jnp.where(
            parity == core, jnp.broadcast_to(mine, (8, LANES)), jnp.broadcast_to(theirs, (8, LANES))
        )


def cross_pairs(core, x, y, own, width):
    count, full = x.shape
    return pl.pallas_call(
        functools.partial(cross_kernel, width),
        out_shape=jax.ShapeDtypeStruct((count // LANES * 8, LANES), jnp.float32),
        in_specs=[pl.BlockSpec(memory_space=pltpu.SMEM)] + [pl.BlockSpec(memory_space=pltpu.VMEM)] * 3,
        out_specs=pl.BlockSpec(memory_space=pltpu.VMEM),
        scratch_shapes=[
            pltpu.VMEM((count, LANES), jnp.float32),
            pltpu.VMEM((8, count), jnp.float32),
            pltpu.VMEM((count, LANES), jnp.float32),
            pltpu.VMEM((8, count), jnp.float32),
        ],
        compiler_params=pltpu.CompilerParams(vmem_limit_bytes=40 * 2**20),
        cost_estimate=pl.CostEstimate(
            flops=count * count * width, bytes_accessed=4 * count * full, transcendentals=0
        ),
        name="cross_pairs",
    )(core, x, y, own)


def pick_kernel(lane_ref, recv_ref, target_ref, out_ref):
    pairs = recv_ref.shape[0]
    owners = pairs // 2
    best = jnp.maximum(
        recv_ref[pl.ds(0, owners, stride=2), :], recv_ref[pl.ds(1, owners, stride=2), :]
    )
    target = target_ref[...]
    rows = target.shape[1]
    cid = target >> 5
    slot = (target & (CAP - 1)) + lane_ref[0]
    chosen = lax.broadcasted_iota(jnp.int32, (owners, rows), 0) == cid
    chosen = chosen.astype(jnp.float32).astype(jnp.bfloat16)
    total = jnp.zeros((LANES, rows), jnp.float32)
    rest = best
    for _ in range(3):
        piece = rest.astype(jnp.bfloat16)
        rest = rest - piece.astype(jnp.float32)
        total += lax.dot_general(
            piece, chosen, (((0,), (0,)), ((), ())), preferred_element_type=jnp.float32
        )
    mine = lax.broadcasted_iota(jnp.int32, (LANES, rows), 0) == slot
    out_ref[...] = jnp.sum(jnp.where(mine, total, 0.0), axis=0, keepdims=True)


def pick(lane, recv, target):
    return pl.pallas_call(
        pick_kernel,
        out_shape=jax.ShapeDtypeStruct(target.shape, jnp.float32),
        in_specs=[pl.BlockSpec(memory_space=pltpu.SMEM)] + [pl.BlockSpec(memory_space=pltpu.VMEM)] * 2,
        out_specs=pl.BlockSpec(memory_space=pltpu.VMEM),
        name="pick_results",
    )(lane, recv, target)


def shards(embeddings, cluster, order):
    owners = lax.axis_size("owner")
    rows, width = embeddings.shape
    packed, target = pack(embeddings, cluster.reshape(1, rows), order.reshape(1, rows), owners)
    received = lax.all_to_all(packed, "owner", split_axis=0, concat_axis=0, tiled=True)
    mine = received.reshape(owners * CAP, width + LANES)
    theirs = lax.ppermute(mine, "split", [(0, 1), (1, 0)])
    own = own_pairs(mine, width)
    core = lax.axis_index("split").astype(jnp.int32).reshape(1)
    best = cross_pairs(core, mine, theirs, own, width)
    returned = lax.all_to_all(best, ("owner", "split"), split_axis=0, concat_axis=0, tiled=True)
    per_row = LANES // CAP
    lane = (lax.axis_index("owner") % per_row * CAP).astype(jnp.int32).reshape(1)
    return pick(lane, returned, target).reshape(rows)


def solution(mesh):
    return jax.shard_map(
        shards,
        mesh=mesh,
        in_specs=(P(("owner", "split"), None), P(("owner", "split"), None), P(("owner", "split"))),
        out_specs=P(("owner", "split")),
        check_vma=False,
    )
```

```python
import functools
import jax
import jax.numpy as jnp
from jax import lax
from jax.experimental import pallas as pl
from jax.experimental.pallas import tpu as pltpu
from jax.sharding import PartitionSpec as P

CAP = 32
LANES = 128
META = 16
EMPTY = 262144.0
TILE = 512
PER_TILE = TILE // CAP
PER_ROW = LANES // CAP


def pack_kernel(emb_hbm, cid_hbm, order_hbm, out_ref, target_ref, emb_ref, cid_ref, order_ref, unit_ref, sems):
    rows, width = emb_ref.shape
    owners = out_ref.shape[0]
    chunk = 128
    chunks = rows // chunk
    small = [
        pltpu.make_async_copy(cid_hbm, cid_ref, sems.at[chunks]),
        pltpu.make_async_copy(order_hbm, order_ref, sems.at[chunks + 1]),
    ]
    loads = []
    for r in range(chunks):
        part = pl.ds(r * chunk, chunk)
        loads.append(pltpu.make_async_copy(emb_hbm.at[part], emb_ref.at[part], sems.at[r]))
    for copy in small + loads:
        copy.start()
    for copy in small:
        copy.wait()
    cid = cid_ref[...].astype(jnp.float32)
    column = jnp.transpose(jnp.broadcast_to(cid, (LANES, rows)))
    above = lax.broadcasted_iota(jnp.int32, (rows, LANES), 0)
    for j in range(rows // LANES):
        lanes = slice(j * LANES, (j + 1) * LANES)
        here = lax.broadcasted_iota(jnp.int32, (rows, LANES), 1) + j * LANES
        same = (column == cid[:, lanes]) & (above < here)
        place = jnp.sum(same.astype(jnp.float32), axis=0, keepdims=True)
        target_ref[:, lanes] = (cid[:, lanes] * CAP + place).astype(jnp.int32)
    code = order_ref[...] + 1
    high = jnp.broadcast_to((code >> 8).astype(jnp.float32), (META // 2, rows))
    low = jnp.broadcast_to((code & 255).astype(jnp.float32), (META // 2, rows))
    both = jnp.concatenate([high, low, jnp.zeros((LANES - META, rows), jnp.float32)], axis=0)
    unit_ref[:, width:] = jnp.transpose(both).astype(jnp.bfloat16)
    for r in range(chunks):
        part = pl.ds(r * chunk, chunk)
        loads[r].wait()
        e = emb_ref[part, :].astype(jnp.float32)
        scale = lax.rsqrt(jnp.sum(e * e, axis=1, keepdims=True) + 1e-06)
        unit_ref[part, :width] = (e * scale).astype(jnp.bfloat16)
    target = target_ref[...]
    me = lax.axis_index("owner") % PER_ROW
    segment = lax.broadcasted_iota(jnp.int32, (META, LANES), 1) // CAP
    for step in range(owners // PER_TILE):
        block = slice(step * PER_TILE, (step + 1) * PER_TILE)
        slot = lax.broadcasted_iota(jnp.int32, (TILE, rows), 0) + step * TILE
        place = (slot == target).astype(jnp.float32).astype(jnp.bfloat16)
        packed = jnp.dot(place, unit_ref[...], preferred_element_type=jnp.float32)
        for k in range(width // LANES):
            part = packed[:, k * LANES : (k + 1) * LANES].astype(jnp.bfloat16)
            out_ref[block, k * CAP : (k + 1) * CAP, :] = part.reshape(PER_TILE, CAP, LANES)
        ranks = jnp.transpose(packed[:, width:])[:META, :]
        for t in range(PER_TILE // PER_ROW):
            tile = ranks[:, t * LANES : (t + 1) * LANES]
            for q in range(PER_ROW):
                alone = jnp.where(segment == q, tile, 0.0)
                moved = pltpu.roll(alone, (me + PER_ROW - q) % PER_ROW * CAP, 1)
                out_ref[step * PER_TILE + t * PER_ROW + q, width // LANES * CAP :, :] = moved.astype(
                    jnp.bfloat16
                )


def pack(embeddings, cid, order, owners):
    rows, width = embeddings.shape
    return pl.pallas_call(
        pack_kernel,
        out_shape=(
            jax.ShapeDtypeStruct((owners, width // LANES * CAP + META, LANES), jnp.bfloat16),
            jax.ShapeDtypeStruct((1, rows), jnp.int32),
        ),
        in_specs=[pl.BlockSpec(memory_space=pl.ANY)] * 3,
        out_specs=(pl.BlockSpec(memory_space=pltpu.VMEM),) * 2,
        scratch_shapes=[
            pltpu.VMEM((rows, width), jnp.bfloat16),
            pltpu.VMEM((1, rows), jnp.int32),
            pltpu.VMEM((1, rows), jnp.int32),
            pltpu.VMEM((rows, width + LANES), jnp.bfloat16),
            pltpu.SemaphoreType.DMA((rows // 128 + 2,)),
        ],
        compiler_params=pltpu.CompilerParams(vmem_limit_bytes=32 * 2**20),
        name="pack_rows",
    )(embeddings, cid, order)


def tile_copies(source, first, target, sems):
    copies = []
    for k in range(target.shape[2] // LANES):
        copies.append(
            pltpu.make_async_copy(
                source.at[pl.ds(first, PER_TILE), pl.ds(k * CAP, CAP), :],
                target.at[:, :, pl.ds(k * LANES, LANES)],
                sems.at[k],
            )
        )
    return copies


def rank_row(meta_ref, group):
    tiles = meta_ref[group * PER_ROW : (group + 1) * PER_ROW].astype(jnp.float32)
    both = jnp.sum(tiles, axis=0)
    code = both[: META // 2] * 256.0 + both[META // 2 :]
    return jnp.where(code == 0.0, EMPTY, code)


def as_column(row):
    return jnp.transpose(jnp.broadcast_to(row[:1], (LANES, LANES)))


def compare(x_ref, y_ref, column_ref, row_ref, rows_ref, columns_ref):
    width = x_ref.shape[2]
    y = y_ref[...].reshape(TILE, width)
    part = TILE // 2
    for h in range(2):
        some = slice(h * part, (h + 1) * part)
        x = x_ref[h * PER_TILE // 2 : (h + 1) * PER_TILE // 2].reshape(part, width)
        sims = lax.dot_general(x, y, (((1,), (1,)), ((), ())), preferred_element_type=jnp.float32)
        column = column_ref[some, :]
        best = rows_ref[some, :]
        for j in range(TILE // LANES):
            lanes = slice(j * LANES, (j + 1) * LANES)
            s = sims[:, lanes]
            earlier = row_ref[:1, lanes] < column
            best = jnp.maximum(best, jnp.where(earlier, s, -1.0))
            if columns_ref is not None:
                later = jnp.where(earlier, -1.0, s)
                across = jnp.max(later.reshape(-1, 8, LANES), axis=0)
                columns_ref[:, lanes] = jnp.maximum(columns_ref[:, lanes], across)
        rows_ref[some, :] = best


def own_kernel(x_hbm, out_ref, x_ref, meta_ref, column_ref, row_ref, rows_ref, columns_ref, sems, meta_sem):
    tiles = x_ref.shape[0]
    meta_row = x_hbm.shape[1] - META
    meta = pltpu.make_async_copy(x_hbm.at[:, pl.ds(meta_row, META), :], meta_ref, meta_sem)
    meta.start()
    loads = [tile_copies(x_hbm, t * PER_TILE, x_ref.at[t], sems.at[t]) for t in range(tiles)]
    for load in loads:
        for copy in load:
            copy.start()
    rows_ref[...] = jnp.full(rows_ref.shape, -1.0, jnp.float32)
    columns_ref[...] = jnp.full(columns_ref.shape, -1.0, jnp.float32)
    meta.wait()
    for j in range(tiles):
        b = slice(j * TILE, (j + 1) * TILE)
        for g in range(j * TILE // LANES, (j + 1) * TILE // LANES):
            lanes = slice(g * LANES, (g + 1) * LANES)
            row = rank_row(meta_ref, g)
            row_ref[:, lanes] = row
            column_ref[lanes, :] = as_column(row)
        for copy in loads[j]:
            copy.wait()
        for i in range(j + 1):
            a = slice(i * TILE, (i + 1) * TILE)
            compare(
                x_ref.at[i], x_ref.at[j], column_ref.at[a], row_ref.at[:, b],
                rows_ref.at[a], columns_ref.at[:, b] if j > i else None,
            )
    for g in range(tiles * TILE // LANES):
        a = slice(g * LANES, (g + 1) * LANES)
        best = jnp.max(jnp.transpose(rows_ref[a, :]), axis=0, keepdims=True)
        best = jnp.maximum(best, jnp.max(columns_ref[:, a], axis=0, keepdims=True))
        out_ref[:, a] = jnp.broadcast_to(best, (8, LANES))


def own_pairs(x, width):
    owners = x.shape[0]
    count = owners * CAP
    tiles = count // TILE
    return pl.pallas_call(
        own_kernel,
        out_shape=jax.ShapeDtypeStruct((8, count), jnp.float32),
        in_specs=[pl.BlockSpec(memory_space=pl.ANY)],
        out_specs=pl.BlockSpec(memory_space=pltpu.VMEM),
        scratch_shapes=[
            pltpu.VMEM((tiles, PER_TILE, CAP, width), jnp.bfloat16),
            pltpu.VMEM((owners, META, LANES), jnp.bfloat16),
            pltpu.VMEM((count, LANES), jnp.float32),
            pltpu.VMEM((8, count), jnp.float32),
            pltpu.VMEM((count, LANES), jnp.float32),
            pltpu.VMEM((8, count), jnp.float32),
            pltpu.SemaphoreType.DMA((tiles, width // LANES)),
            pltpu.SemaphoreType.DMA(()),
        ],
        compiler_params=pltpu.CompilerParams(vmem_limit_bytes=32 * 2**20),
        cost_estimate=pl.CostEstimate(
            flops=count * (count + TILE) * width, bytes_accessed=2 * count * width, transcendentals=0
        ),
        name="own_pairs",
    )(x)


def cross_kernel(x_hbm, y_hbm, own_ref, out_ref, a_ref, b_ref, a_meta, b_meta, column_ref, row_ref, rows_ref, columns_ref, a_sems, b_sems, meta_sems):
    core = lax.axis_index("split")
    tiles, halves = a_ref.shape[0], b_ref.shape[0]
    meta_row = x_hbm.shape[1] - META
    half = halves * PER_TILE

    def copies(all_hbm, some_hbm, first):
        metas = [
            pltpu.make_async_copy(all_hbm.at[:, pl.ds(meta_row, META), :], a_meta, meta_sems.at[0]),
            pltpu.make_async_copy(
                some_hbm.at[pl.ds(first, half), pl.ds(meta_row, META), :], b_meta, meta_sems.at[1]
            ),
        ]
        a = [tile_copies(all_hbm, t * PER_TILE, a_ref.at[t], a_sems.at[t]) for t in range(tiles)]
        b = [tile_copies(some_hbm, first + t * PER_TILE, b_ref.at[t], b_sems.at[t]) for t in range(halves)]
        return metas, a, b

    def start(metas, a, b):
        for copy in metas + b[0] + a[0]:
            copy.start()
        for load in b[1:] + a[1:]:
            for copy in load:
                copy.start()

    @pl.when(core == 0)
    def _():
        start(*copies(x_hbm, y_hbm, 0))

    @pl.when(core != 0)
    def _():
        start(*copies(y_hbm, x_hbm, half))

    metas, a_loads, b_loads = copies(x_hbm, y_hbm, 0)
    rows_ref[...] = jnp.full(rows_ref.shape, -1.0, jnp.float32)
    columns_ref[...] = jnp.full(columns_ref.shape, -1.0, jnp.float32)
    for copy in metas:
        copy.wait()
    for g in range(tiles * TILE // LANES):
        lanes = slice(g * LANES, (g + 1) * LANES)
        column_ref[lanes, :] = as_column(rank_row(a_meta, g))
    for g in range(halves * TILE // LANES):
        row_ref[:, g * LANES : (g + 1) * LANES] = rank_row(b_meta, g)
    for copy in b_loads[0]:
        copy.wait()
    for i in range(tiles):
        a = slice(i * TILE, (i + 1) * TILE)
        for copy in a_loads[i]:
            copy.wait()
        for j in range(halves):
            b = slice(j * TILE, (j + 1) * TILE)
            if i == 0 and j > 0:
                for copy in b_loads[j]:
                    copy.wait()
            compare(
                a_ref.at[i], b_ref.at[j], column_ref.at[a], row_ref.at[:, b],
                rows_ref.at[a], columns_ref.at[:, b],
            )
    parity = lax.broadcasted_iota(jnp.int32, (8, LANES), 0) % 2
    groups = tiles * TILE // LANES
    cut = groups - halves * TILE // LANES
    nothing = jnp.full((1, LANES), -1.0, jnp.float32)
    for g in range(groups):
        a = slice(g * LANES, (g + 1) * LANES)
        from_all = jnp.max(jnp.transpose(rows_ref[a, :]), axis=0, keepdims=True)
        low = high = nothing
        if g < groups - cut:
            low = jnp.max(columns_ref[:, a], axis=0, keepdims=True)
        if g >= cut:
            b = slice((g - cut) * LANES, (g - cut + 1) * LANES)
            high = jnp.max(columns_ref[:, b], axis=0, keepdims=True)
        mine = jnp.maximum(own_ref[:1, a], jnp.where(core == 0, from_all, high))
        theirs = jnp.where(core == 0, low, from_all)
        out_ref[g * 8 : (g + 1) * 8, :] = jnp.where(
            parity == core, jnp.broadcast_to(mine, (8, LANES)), jnp.broadcast_to(theirs, (8, LANES))
        )


def cross_pairs(x, y, own, width):
    owners = x.shape[0]
    count = owners * CAP
    tiles = count // TILE
    halves = tiles // 2
    return pl.pallas_call(
        cross_kernel,
        out_shape=jax.ShapeDtypeStruct((count // LANES * 8, LANES), jnp.float32),
        in_specs=[pl.BlockSpec(memory_space=pl.ANY)] * 2 + [pl.BlockSpec(memory_space=pltpu.VMEM)],
        out_specs=pl.BlockSpec(memory_space=pltpu.VMEM),
        scratch_shapes=[
            pltpu.VMEM((tiles, PER_TILE, CAP, width), jnp.bfloat16),
            pltpu.VMEM((halves, PER_TILE, CAP, width), jnp.bfloat16),
            pltpu.VMEM((owners, META, LANES), jnp.bfloat16),
            pltpu.VMEM((owners // 2, META, LANES), jnp.bfloat16),
            pltpu.VMEM((count, LANES), jnp.float32),
            pltpu.VMEM((8, count // 2), jnp.float32),
            pltpu.VMEM((count, LANES), jnp.float32),
            pltpu.VMEM((8, count // 2), jnp.float32),
            pltpu.SemaphoreType.DMA((tiles, width // LANES)),
            pltpu.SemaphoreType.DMA((halves, width // LANES)),
            pltpu.SemaphoreType.DMA((2,)),
        ],
        compiler_params=pltpu.CompilerParams(vmem_limit_bytes=32 * 2**20),
        cost_estimate=pl.CostEstimate(
            flops=count * count * width, bytes_accessed=3 * count * width, transcendentals=0
        ),
        name="cross_pairs",
    )(x, y, own)


def pick_kernel(recv_ref, target_ref, out_ref):
    pairs = recv_ref.shape[0]
    owners = pairs // 2
    best = jnp.maximum(
        recv_ref[pl.ds(0, owners, stride=2), :], recv_ref[pl.ds(1, owners, stride=2), :]
    )
    target = target_ref[...]
    rows = target.shape[1]
    cid = target >> 5
    slot = (target & (CAP - 1)) + lax.axis_index("owner") % PER_ROW * CAP
    chosen = lax.broadcasted_iota(jnp.int32, (owners, rows), 0) == cid
    chosen = chosen.astype(jnp.float32).astype(jnp.bfloat16)
    total = jnp.zeros((LANES, rows), jnp.float32)
    rest = best
    for _ in range(3):
        piece = rest.astype(jnp.bfloat16)
        rest = rest - piece.astype(jnp.float32)
        total += lax.dot_general(
            piece, chosen, (((0,), (0,)), ((), ())), preferred_element_type=jnp.float32
        )
    mine = lax.broadcasted_iota(jnp.int32, (LANES, rows), 0) == slot
    out_ref[...] = jnp.sum(jnp.where(mine, total, 0.0), axis=0, keepdims=True)


def pick(recv, target):
    return pl.pallas_call(
        pick_kernel,
        out_shape=jax.ShapeDtypeStruct(target.shape, jnp.float32),
        in_specs=[pl.BlockSpec(memory_space=pltpu.VMEM)] * 2,
        out_specs=pl.BlockSpec(memory_space=pltpu.VMEM),
        compiler_params=pltpu.CompilerParams(vmem_limit_bytes=8 * 2**20),
        name="pick_results",
    )(recv, target)


def shards(embeddings, cluster, order):
    owners = lax.axis_size("owner")
    rows, width = embeddings.shape
    packed, target = pack(embeddings, cluster.reshape(1, rows), order.reshape(1, rows), owners)
    mine = lax.all_to_all(packed, "owner", split_axis=0, concat_axis=0, tiled=True)
    theirs = lax.ppermute(mine, "split", [(0, 1), (1, 0)])
    own = own_pairs(mine, width)
    best = cross_pairs(mine, theirs, own, width)
    returned = lax.all_to_all(best, ("owner", "split"), split_axis=0, concat_axis=0, tiled=True)
    return pick(returned, target).reshape(rows)


def solution(mesh):
    return jax.shard_map(
        shards,
        mesh=mesh,
        in_specs=(P(("owner", "split"), None), P(("owner", "split"), None), P(("owner", "split"))),
        out_specs=P(("owner", "split")),
        check_vma=False,
    )
```

```python
import functools
import jax
import jax.numpy as jnp
from jax import lax
from jax.experimental import pallas as pl
from jax.experimental.pallas import tpu as pltpu
from jax.sharding import PartitionSpec as P

CAP = 32
LANES = 128
META = 16
EMPTY = 262144.0
TILE = 512
PART = 512
PER_TILE = TILE // CAP
PER_ROW = LANES // CAP


def pack_kernel(emb_hbm, cid_hbm, order_hbm, out_ref, target_ref, emb_ref, cid_ref, order_ref, unit_ref, sems):
    rows, width = emb_ref.shape
    owners = out_ref.shape[0]
    chunk = 128
    chunks = rows // chunk
    small = [
        pltpu.make_async_copy(cid_hbm, cid_ref, sems.at[chunks]),
        pltpu.make_async_copy(order_hbm, order_ref, sems.at[chunks + 1]),
    ]
    loads = []
    for r in range(chunks):
        part = pl.ds(r * chunk, chunk)
        loads.append(pltpu.make_async_copy(emb_hbm.at[part], emb_ref.at[part], sems.at[r]))
    for copy in small + loads:
        copy.start()
    for copy in small:
        copy.wait()
    cid = cid_ref[...].astype(jnp.float32)
    column = jnp.transpose(jnp.broadcast_to(cid, (LANES, rows)))
    above = lax.broadcasted_iota(jnp.int32, (rows, LANES), 0)
    for j in range(rows // LANES):
        lanes = slice(j * LANES, (j + 1) * LANES)
        here = lax.broadcasted_iota(jnp.int32, (rows, LANES), 1) + j * LANES
        same = (column == cid[:, lanes]) & (above < here)
        place = jnp.sum(same.astype(jnp.float32), axis=0, keepdims=True)
        target_ref[:, lanes] = (cid[:, lanes] * CAP + place).astype(jnp.int32)
    code = order_ref[...] + 1
    high = jnp.broadcast_to((code >> 8).astype(jnp.float32), (META // 2, rows))
    low = jnp.broadcast_to((code & 255).astype(jnp.float32), (META // 2, rows))
    both = jnp.concatenate([high, low, jnp.zeros((LANES - META, rows), jnp.float32)], axis=0)
    unit_ref[:, width:] = jnp.transpose(both).astype(jnp.bfloat16)
    for r in range(chunks):
        part = pl.ds(r * chunk, chunk)
        loads[r].wait()
        e = emb_ref[part, :].astype(jnp.float32)
        scale = lax.rsqrt(jnp.sum(e * e, axis=1, keepdims=True) + 1e-06)
        unit_ref[part, :width] = (e * scale).astype(jnp.bfloat16)
    target = target_ref[...]
    me = lax.axis_index("owner") % PER_ROW
    segment = lax.broadcasted_iota(jnp.int32, (META, LANES), 1) // CAP
    for step in range(owners // PER_TILE):
        block = slice(step * PER_TILE, (step + 1) * PER_TILE)
        slot = lax.broadcasted_iota(jnp.int32, (TILE, rows), 0) + step * TILE
        place = (slot == target).astype(jnp.float32).astype(jnp.bfloat16)
        packed = jnp.dot(place, unit_ref[...], preferred_element_type=jnp.float32)
        for k in range(width // LANES):
            part = packed[:, k * LANES : (k + 1) * LANES].astype(jnp.bfloat16)
            out_ref[block, k * CAP : (k + 1) * CAP, :] = part.reshape(PER_TILE, CAP, LANES)
        ranks = jnp.transpose(packed[:, width:])[:META, :]
        for t in range(PER_TILE // PER_ROW):
            tile = ranks[:, t * LANES : (t + 1) * LANES]
            for q in range(PER_ROW):
                alone = jnp.where(segment == q, tile, 0.0)
                moved = pltpu.roll(alone, (me + PER_ROW - q) % PER_ROW * CAP, 1)
                out_ref[step * PER_TILE + t * PER_ROW + q, width // LANES * CAP :, :] = moved.astype(
                    jnp.bfloat16
                )


def pack(embeddings, cid, order, owners):
    rows, width = embeddings.shape
    return pl.pallas_call(
        pack_kernel,
        out_shape=(
            jax.ShapeDtypeStruct((owners, width // LANES * CAP + META, LANES), jnp.bfloat16),
            jax.ShapeDtypeStruct((1, rows), jnp.int32),
        ),
        in_specs=[pl.BlockSpec(memory_space=pl.ANY)] * 3,
        out_specs=(pl.BlockSpec(memory_space=pltpu.VMEM),) * 2,
        scratch_shapes=[
            pltpu.VMEM((rows, width), jnp.bfloat16),
            pltpu.VMEM((1, rows), jnp.int32),
            pltpu.VMEM((1, rows), jnp.int32),
            pltpu.VMEM((rows, width + LANES), jnp.bfloat16),
            pltpu.SemaphoreType.DMA((rows // 128 + 2,)),
        ],
        compiler_params=pltpu.CompilerParams(vmem_limit_bytes=32 * 2**20),
        name="pack_rows",
    )(embeddings, cid, order)


def rank_row(x_ref, group):
    meta = x_ref.shape[1] - META
    tiles = x_ref[group * PER_ROW : (group + 1) * PER_ROW, meta:, :].astype(jnp.float32)
    both = jnp.sum(tiles, axis=0)
    code = both[: META // 2] * 256.0 + both[META // 2 :]
    return jnp.where(code == 0.0, EMPTY, code)


def as_column(row):
    return jnp.transpose(jnp.broadcast_to(row[:1], (LANES, LANES)))


def rows_of(x_ref, first, count):
    block = slice(first // CAP, (first + count) // CAP)
    columns = (x_ref.shape[1] - META) // CAP
    parts = [x_ref[block, k * CAP : (k + 1) * CAP, :].reshape(count, LANES) for k in range(columns)]
    return jnp.concatenate(parts, axis=1)


def compare(x, y, first, start, column_ref, row_ref, rows_ref, across):
    sims = lax.dot_general(x, y, (((1,), (1,)), ((), ())), preferred_element_type=jnp.float32)
    some = slice(first, first + x.shape[0])
    column = column_ref[some, :]
    best = rows_ref[some, :]
    for j in range(y.shape[0] // LANES):
        s = sims[:, j * LANES : (j + 1) * LANES]
        earlier = row_ref[:1, start + j * LANES : start + (j + 1) * LANES] < column
        best = jnp.maximum(best, jnp.where(earlier, s, -1.0))
        if across[j] is not None:
            later = jnp.where(earlier, -1.0, s)
            across[j] = jnp.maximum(across[j], jnp.max(later.reshape(-1, 8, LANES), axis=0))
    rows_ref[some, :] = best


def lowest():
    return jnp.full((8, LANES), -1.0, jnp.float32)


def own_kernel(x_ref, out_ref, column_ref, row_ref, rows_ref, columns_ref):
    count = x_ref.shape[0] * CAP
    rows_ref[...] = jnp.full(rows_ref.shape, -1.0, jnp.float32)
    for g in range(count // LANES):
        lanes = slice(g * LANES, (g + 1) * LANES)
        row = rank_row(x_ref, g)
        row_ref[:, lanes] = row
        column_ref[lanes, :] = as_column(row)
    per = TILE // LANES
    for start in range(0, count, TILE):
        y = rows_of(x_ref, start, TILE)
        across = [lowest() for _ in range(per)]
        for first in range(0, start, PART):
            x = rows_of(x_ref, first, PART)
            compare(x, y, first, start, column_ref, row_ref, rows_ref, across)
        half = per // 2
        x = rows_of(x_ref, start, TILE // 2)
        some = [None] * half + across[half:]
        compare(x, y, start, start, column_ref, row_ref, rows_ref, some)
        across[half:] = some[half:]
        middle = start + TILE // 2
        x = rows_of(x_ref, middle, TILE // 2)
        compare(x, x, middle, middle, column_ref, row_ref, rows_ref, [None] * half)
        for j in range(per):
            columns_ref[:, start + j * LANES : start + (j + 1) * LANES] = across[j]
    for g in range(count // LANES):
        a = slice(g * LANES, (g + 1) * LANES)
        best = jnp.max(jnp.transpose(rows_ref[a, :]), axis=0, keepdims=True)
        best = jnp.maximum(best, jnp.max(columns_ref[:, a], axis=0, keepdims=True))
        out_ref[:, a] = jnp.broadcast_to(best, (8, LANES))


def own_pairs(x, width):
    owners = x.shape[0]
    count = owners * CAP
    return pl.pallas_call(
        own_kernel,
        out_shape=jax.ShapeDtypeStruct((8, count), jnp.float32),
        in_specs=[pl.BlockSpec(memory_space=pltpu.VMEM)],
        out_specs=pl.BlockSpec(memory_space=pltpu.VMEM),
        scratch_shapes=[
            pltpu.VMEM((count, LANES), jnp.float32),
            pltpu.VMEM((8, count), jnp.float32),
            pltpu.VMEM((count, LANES), jnp.float32),
            pltpu.VMEM((8, count), jnp.float32),
        ],
        compiler_params=pltpu.CompilerParams(vmem_limit_bytes=24 * 2**20),
        cost_estimate=pl.CostEstimate(
            flops=count * (count + TILE) * width, bytes_accessed=2 * count * width, transcendentals=0
        ),
        name="own_pairs",
    )(x)


def cross_kernel(x_ref, y_ref, own_ref, out_ref, column_ref, row_ref, rows_ref, columns_ref):
    core = lax.axis_index("split")
    count = x_ref.shape[0] * CAP
    half = count // 2
    rows_ref[...] = jnp.full(rows_ref.shape, -1.0, jnp.float32)

    def pairs(all_ref, some_ref):
        for g in range(count // LANES):
            column_ref[g * LANES : (g + 1) * LANES, :] = as_column(rank_row(all_ref, g))
        for g in range(half // LANES):
            row_ref[:, g * LANES : (g + 1) * LANES] = rank_row(some_ref, g)
        for start in range(0, half, TILE):
            y = rows_of(some_ref, start, TILE)
            across = [lowest() for _ in range(TILE // LANES)]
            for first in range(0, count, PART):
                x = rows_of(all_ref, first, PART)
                compare(x, y, first, start, column_ref, row_ref, rows_ref, across)
            for j, best in enumerate(across):
                columns_ref[:, start + j * LANES : start + (j + 1) * LANES] = best

    @pl.when(core == 0)
    def _():
        pairs(x_ref, y_ref.at[: half // CAP])

    @pl.when(core != 0)
    def _():
        pairs(y_ref, x_ref.at[half // CAP :])

    parity = lax.broadcasted_iota(jnp.int32, (8, LANES), 0) % 2
    groups = count // LANES
    nothing = jnp.full((1, LANES), -1.0, jnp.float32)
    for g in range(groups):
        a = slice(g * LANES, (g + 1) * LANES)
        from_all = jnp.max(jnp.transpose(rows_ref[a, :]), axis=0, keepdims=True)
        b = slice(g % (groups // 2) * LANES, (g % (groups // 2) + 1) * LANES)
        from_half = jnp.max(columns_ref[:, b], axis=0, keepdims=True)
        low, high = (from_half, nothing) if g < groups // 2 else (nothing, from_half)
        mine = jnp.maximum(own_ref[:1, a], jnp.where(core == 0, from_all, high))
        theirs = jnp.where(core == 0, low, from_all)
        out_ref[g * 8 : (g + 1) * 8, :] = jnp.where(
            parity == core, jnp.broadcast_to(mine, (8, LANES)), jnp.broadcast_to(theirs, (8, LANES))
        )


def cross_pairs(x, y, own, width):
    owners = x.shape[0]
    count = owners * CAP
    return pl.pallas_call(
        cross_kernel,
        out_shape=jax.ShapeDtypeStruct((count // LANES * 8, LANES), jnp.float32),
        in_specs=[pl.BlockSpec(memory_space=pltpu.VMEM)] * 3,
        out_specs=pl.BlockSpec(memory_space=pltpu.VMEM),
        scratch_shapes=[
            pltpu.VMEM((count, LANES), jnp.float32),
            pltpu.VMEM((8, count // 2), jnp.float32),
            pltpu.VMEM((count, LANES), jnp.float32),
            pltpu.VMEM((8, count // 2), jnp.float32),
        ],
        compiler_params=pltpu.CompilerParams(vmem_limit_bytes=24 * 2**20),
        cost_estimate=pl.CostEstimate(
            flops=count * count * width, bytes_accessed=3 * count * width, transcendentals=0
        ),
        name="cross_pairs",
    )(x, y, own)


def pick_kernel(recv_ref, target_ref, out_ref):
    pairs = recv_ref.shape[0]
    owners = pairs // 2
    best = jnp.maximum(
        recv_ref[pl.ds(0, owners, stride=2), :], recv_ref[pl.ds(1, owners, stride=2), :]
    )
    target = target_ref[...]
    rows = target.shape[1]
    cid = target >> 5
    slot = (target & (CAP - 1)) + lax.axis_index("owner") % PER_ROW * CAP
    chosen = lax.broadcasted_iota(jnp.int32, (owners, rows), 0) == cid
    chosen = chosen.astype(jnp.float32).astype(jnp.bfloat16)
    total = jnp.zeros((LANES, rows), jnp.float32)
    rest = best
    for _ in range(3):
        piece = rest.astype(jnp.bfloat16)
        rest = rest - piece.astype(jnp.float32)
        total += lax.dot_general(
            piece, chosen, (((0,), (0,)), ((), ())), preferred_element_type=jnp.float32
        )
    mine = lax.broadcasted_iota(jnp.int32, (LANES, rows), 0) == slot
    out_ref[...] = jnp.sum(jnp.where(mine, total, 0.0), axis=0, keepdims=True)


def pick(recv, target):
    return pl.pallas_call(
        pick_kernel,
        out_shape=jax.ShapeDtypeStruct(target.shape, jnp.float32),
        in_specs=[pl.BlockSpec(memory_space=pltpu.VMEM)] * 2,
        out_specs=pl.BlockSpec(memory_space=pltpu.VMEM),
        compiler_params=pltpu.CompilerParams(vmem_limit_bytes=8 * 2**20),
        name="pick_results",
    )(recv, target)


def shards(embeddings, cluster, order):
    owners = lax.axis_size("owner")
    rows, width = embeddings.shape
    packed, target = pack(embeddings, cluster.reshape(1, rows), order.reshape(1, rows), owners)
    mine = lax.all_to_all(packed, "owner", split_axis=0, concat_axis=0, tiled=True)
    theirs = lax.ppermute(mine, "split", [(0, 1), (1, 0)])
    own = own_pairs(mine, width)
    best = cross_pairs(mine, theirs, own, width)
    returned = lax.all_to_all(best, ("owner", "split"), split_axis=0, concat_axis=0, tiled=True)
    return pick(returned, target).reshape(rows)


def solution(mesh):
    return jax.shard_map(
        shards,
        mesh=mesh,
        in_specs=(P(("owner", "split"), None), P(("owner", "split"), None), P(("owner", "split"))),
        out_specs=P(("owner", "split")),
        check_vma=False,
    )
```

```python
import functools
import jax
import jax.numpy as jnp
from jax import lax
from jax.experimental import pallas as pl
from jax.experimental.pallas import tpu as pltpu
from jax.sharding import PartitionSpec as P

CAP = 32
LANES = 128
META = 8
EMPTY = 262144.0
TILE = 512
PART = 512
PER_TILE = TILE // CAP
PER_ROW = LANES // CAP


def pack_kernel(emb_ref, code_ref, out_ref, target_ref, unit_ref):
    rows, width = emb_ref.shape
    owners = out_ref.shape[0]
    code = code_ref[...]
    cid = (code >> 16).astype(jnp.float32)
    column = jnp.transpose(jnp.broadcast_to(cid, (LANES, rows)))
    above = lax.broadcasted_iota(jnp.int32, (LANES, LANES), 0)
    here = lax.broadcasted_iota(jnp.int32, (LANES, LANES), 1)
    for j in range(rows // LANES):
        lanes = slice(j * LANES, (j + 1) * LANES)
        place = jnp.zeros((1, LANES), jnp.float32)
        for i in range(j + 1):
            same = column[i * LANES : (i + 1) * LANES] == cid[:, lanes]
            if i == j:
                same = same & (above < here)
            place += jnp.sum(jnp.where(same, 1.0, 0.0), axis=0, keepdims=True)
        target_ref[:, lanes] = (cid[:, lanes] * CAP + place).astype(jnp.int32)
    rank = (code & 65535) + 1
    high = jnp.broadcast_to((rank >> 8).astype(jnp.float32), (META // 2, rows))
    low = jnp.broadcast_to((rank & 255).astype(jnp.float32), (META // 2, rows))
    both = jnp.concatenate([high, low, jnp.zeros((LANES - META, rows), jnp.float32)], axis=0)
    unit_ref[:, width:] = jnp.transpose(both).astype(jnp.bfloat16)
    chunk = 128
    for r in range(rows // chunk):
        part = slice(r * chunk, (r + 1) * chunk)
        e = emb_ref[part, :].astype(jnp.float32)
        scale = lax.rsqrt(jnp.sum(e * e, axis=1, keepdims=True) + 1e-06)
        unit_ref[part, :width] = (e * scale).astype(jnp.bfloat16)
    target = target_ref[...]
    me = lax.axis_index("owner") % PER_ROW
    segment = lax.broadcasted_iota(jnp.int32, (META, LANES), 1) // CAP
    for step in range(owners // PER_TILE):
        block = slice(step * PER_TILE, (step + 1) * PER_TILE)
        slot = lax.broadcasted_iota(jnp.int32, (TILE, rows), 0)
        place = jnp.where(slot == target - step * TILE, 1.0, 0.0).astype(jnp.bfloat16)
        packed = jnp.dot(place, unit_ref[...], preferred_element_type=jnp.float32)
        for k in range(width // LANES):
            part = packed[:, k * LANES : (k + 1) * LANES].astype(jnp.bfloat16)
            out_ref[block, k * CAP : (k + 1) * CAP, :] = part.reshape(PER_TILE, CAP, LANES)
        ranks = jnp.transpose(packed[:, width:])[:META, :]
        for t in range(PER_TILE // PER_ROW):
            tile = ranks[:, t * LANES : (t + 1) * LANES]
            for q in range(PER_ROW):
                alone = jnp.where(segment == q, tile, 0.0)
                moved = pltpu.roll(alone, (me + PER_ROW - q) % PER_ROW * CAP, 1)
                out_ref[step * PER_TILE + t * PER_ROW + q, width // LANES * CAP :, :] = moved.astype(
                    jnp.bfloat16
                )


def pack(embeddings, code, owners):
    rows, width = embeddings.shape
    return pl.pallas_call(
        pack_kernel,
        out_shape=(
            jax.ShapeDtypeStruct((owners, width // LANES * CAP + META, LANES), jnp.bfloat16),
            jax.ShapeDtypeStruct((1, rows), jnp.int32),
        ),
        in_specs=[pl.BlockSpec(memory_space=pltpu.VMEM)] * 2,
        out_specs=(pl.BlockSpec(memory_space=pltpu.VMEM),) * 2,
        scratch_shapes=[pltpu.VMEM((rows, width + LANES), jnp.bfloat16)],
        compiler_params=pltpu.CompilerParams(vmem_limit_bytes=24 * 2**20),
        name="pack_rows",
    )(embeddings, code)


def rank_row(x_ref, group):
    meta = x_ref.shape[1] - META
    tiles = x_ref[group * PER_ROW : (group + 1) * PER_ROW, meta:, :].astype(jnp.float32)
    both = jnp.sum(tiles, axis=0)
    code = both[:1] * 256.0 + both[META // 2 : META // 2 + 1]
    return jnp.broadcast_to(jnp.where(code == 0.0, EMPTY, code), (8, LANES))


def as_column(row):
    return jnp.transpose(jnp.broadcast_to(row[:1], (LANES, LANES)))


def rows_of(x_ref, first, count):
    block = slice(first // CAP, (first + count) // CAP)
    columns = (x_ref.shape[1] - META) // CAP
    parts = [x_ref[block, k * CAP : (k + 1) * CAP, :].reshape(count, LANES) for k in range(columns)]
    return jnp.concatenate(parts, axis=1)


def compare(x, y, first, start, column_ref, row_ref, rows_ref, across):
    sims = lax.dot_general(x, y, (((1,), (1,)), ((), ())), preferred_element_type=jnp.float32)
    some = slice(first, first + x.shape[0])
    column = column_ref[some, :]
    best = rows_ref[some, :]
    for j in range(y.shape[0] // LANES):
        s = sims[:, j * LANES : (j + 1) * LANES]
        earlier = row_ref[:1, start + j * LANES : start + (j + 1) * LANES] < column
        best = jnp.maximum(best, jnp.where(earlier, s, -1.0))
        if across[j] is not None:
            later = jnp.where(earlier, -1.0, s)
            across[j] = jnp.maximum(across[j], jnp.max(later.reshape(-1, 8, LANES), axis=0))
    rows_ref[some, :] = best


def lowest():
    return jnp.full((8, LANES), -1.0, jnp.float32)


def own_kernel(x_ref, out_ref, column_ref, row_ref, rows_ref, columns_ref):
    count = x_ref.shape[0] * CAP
    rows_ref[...] = jnp.full(rows_ref.shape, -1.0, jnp.float32)
    for g in range(count // LANES):
        lanes = slice(g * LANES, (g + 1) * LANES)
        row = rank_row(x_ref, g)
        row_ref[:, lanes] = row
        column_ref[lanes, :] = as_column(row)
    per = TILE // LANES
    for start in range(0, count, TILE):
        y = rows_of(x_ref, start, TILE)
        across = [lowest() for _ in range(per)]
        for first in range(0, start, PART):
            x = rows_of(x_ref, first, PART)
            compare(x, y, first, start, column_ref, row_ref, rows_ref, across)
        half = per // 2
        x = rows_of(x_ref, start, TILE // 2)
        some = [None] * half + across[half:]
        compare(x, y, start, start, column_ref, row_ref, rows_ref, some)
        across[half:] = some[half:]
        middle = start + TILE // 2
        x = rows_of(x_ref, middle, TILE // 2)
        compare(x, x, middle, middle, column_ref, row_ref, rows_ref, [None] * half)
        for j in range(per):
            columns_ref[:, start + j * LANES : start + (j + 1) * LANES] = across[j]
    for g in range(count // LANES):
        a = slice(g * LANES, (g + 1) * LANES)
        best = jnp.max(jnp.transpose(rows_ref[a, :]), axis=0, keepdims=True)
        best = jnp.maximum(best, jnp.max(columns_ref[:, a], axis=0, keepdims=True))
        out_ref[:, a] = jnp.broadcast_to(best, (8, LANES))


def own_pairs(x, width):
    owners = x.shape[0]
    count = owners * CAP
    return pl.pallas_call(
        own_kernel,
        out_shape=jax.ShapeDtypeStruct((8, count), jnp.float32),
        in_specs=[pl.BlockSpec(memory_space=pltpu.VMEM)],
        out_specs=pl.BlockSpec(memory_space=pltpu.VMEM),
        scratch_shapes=[
            pltpu.VMEM((count, LANES), jnp.float32),
            pltpu.VMEM((8, count), jnp.float32),
            pltpu.VMEM((count, LANES), jnp.float32),
            pltpu.VMEM((8, count), jnp.float32),
        ],
        compiler_params=pltpu.CompilerParams(vmem_limit_bytes=24 * 2**20),
        cost_estimate=pl.CostEstimate(
            flops=count * (count + TILE) * width, bytes_accessed=2 * count * width, transcendentals=0
        ),
        name="own_pairs",
    )(x)


def cross_kernel(x_ref, y_ref, own_ref, out_ref, column_ref, row_ref, rows_ref, columns_ref):
    core = lax.axis_index("split")
    count = x_ref.shape[0] * CAP
    half = count // 2
    rows_ref[...] = jnp.full(rows_ref.shape, -1.0, jnp.float32)

    def pairs(all_ref, some_ref):
        for g in range(count // LANES):
            column_ref[g * LANES : (g + 1) * LANES, :] = as_column(rank_row(all_ref, g))
        for g in range(half // LANES):
            row_ref[:, g * LANES : (g + 1) * LANES] = rank_row(some_ref, g)
        for start in range(0, half, TILE):
            y = rows_of(some_ref, start, TILE)
            across = [lowest() for _ in range(TILE // LANES)]
            for first in range(0, count, PART):
                x = rows_of(all_ref, first, PART)
                compare(x, y, first, start, column_ref, row_ref, rows_ref, across)
            for j, best in enumerate(across):
                columns_ref[:, start + j * LANES : start + (j + 1) * LANES] = best

    @pl.when(core == 0)
    def _():
        pairs(x_ref, y_ref.at[: half // CAP])

    @pl.when(core != 0)
    def _():
        pairs(y_ref, x_ref.at[half // CAP :])

    parity = lax.broadcasted_iota(jnp.int32, (8, LANES), 0) % 2
    groups = count // LANES
    nothing = jnp.full((1, LANES), -1.0, jnp.float32)
    for g in range(groups):
        a = slice(g * LANES, (g + 1) * LANES)
        from_all = jnp.max(jnp.transpose(rows_ref[a, :]), axis=0, keepdims=True)
        b = slice(g % (groups // 2) * LANES, (g % (groups // 2) + 1) * LANES)
        from_half = jnp.max(columns_ref[:, b], axis=0, keepdims=True)
        low, high = (from_half, nothing) if g < groups // 2 else (nothing, from_half)
        mine = jnp.maximum(own_ref[:1, a], jnp.where(core == 0, from_all, high))
        theirs = jnp.where(core == 0, low, from_all)
        out_ref[g * 8 : (g + 1) * 8, :] = jnp.where(
            parity == core, jnp.broadcast_to(mine, (8, LANES)), jnp.broadcast_to(theirs, (8, LANES))
        )


def cross_pairs(x, y, own, width):
    owners = x.shape[0]
    count = owners * CAP
    return pl.pallas_call(
        cross_kernel,
        out_shape=jax.ShapeDtypeStruct((count // LANES * 8, LANES), jnp.float32),
        in_specs=[pl.BlockSpec(memory_space=pltpu.VMEM)] * 3,
        out_specs=pl.BlockSpec(memory_space=pltpu.VMEM),
        scratch_shapes=[
            pltpu.VMEM((count, LANES), jnp.float32),
            pltpu.VMEM((8, count // 2), jnp.float32),
            pltpu.VMEM((count, LANES), jnp.float32),
            pltpu.VMEM((8, count // 2), jnp.float32),
        ],
        compiler_params=pltpu.CompilerParams(vmem_limit_bytes=24 * 2**20),
        cost_estimate=pl.CostEstimate(
            flops=count * count * width, bytes_accessed=3 * count * width, transcendentals=0
        ),
        name="cross_pairs",
    )(x, y, own)


def pick_kernel(recv_ref, target_ref, out_ref):
    pairs = recv_ref.shape[0]
    owners = pairs // 2
    best = jnp.maximum(
        recv_ref[pl.ds(0, owners, stride=2), :], recv_ref[pl.ds(1, owners, stride=2), :]
    )
    target = target_ref[...]
    rows = target.shape[1]
    cid = target >> 5
    slot = (target & (CAP - 1)) + lax.axis_index("owner") % PER_ROW * CAP
    chosen = lax.broadcasted_iota(jnp.int32, (owners, rows), 0) == cid
    chosen = chosen.astype(jnp.float32).astype(jnp.bfloat16)
    total = jnp.zeros((LANES, rows), jnp.float32)
    rest = best
    for _ in range(3):
        piece = rest.astype(jnp.bfloat16)
        rest = rest - piece.astype(jnp.float32)
        total += lax.dot_general(
            piece, chosen, (((0,), (0,)), ((), ())), preferred_element_type=jnp.float32
        )
    mine = lax.broadcasted_iota(jnp.int32, (LANES, rows), 0) == slot
    out_ref[...] = jnp.sum(jnp.where(mine, total, 0.0), axis=0, keepdims=True)


def pick(recv, target):
    return pl.pallas_call(
        pick_kernel,
        out_shape=jax.ShapeDtypeStruct(target.shape, jnp.float32),
        in_specs=[pl.BlockSpec(memory_space=pltpu.VMEM)] * 2,
        out_specs=pl.BlockSpec(memory_space=pltpu.VMEM),
        compiler_params=pltpu.CompilerParams(vmem_limit_bytes=8 * 2**20),
        name="pick_results",
    )(recv, target)


def shards(embeddings, cluster, order):
    owners = lax.axis_size("owner")
    rows, width = embeddings.shape
    cid, rank = lax.optimization_barrier((cluster.reshape(1, rows), order.reshape(1, rows)))
    code = cid * 65536 + rank
    packed, target = pack(embeddings, code, owners)
    mine = lax.all_to_all(packed, "owner", split_axis=0, concat_axis=0, tiled=True)
    theirs = lax.ppermute(mine, "split", [(0, 1), (1, 0)])
    own = own_pairs(mine, width)
    best = cross_pairs(mine, theirs, own, width)
    returned = lax.all_to_all(best, ("owner", "split"), split_axis=0, concat_axis=0, tiled=True)
    return pick(returned, target).reshape(rows)


def solution(mesh):
    return jax.shard_map(
        shards,
        mesh=mesh,
        in_specs=(P(("owner", "split"), None), P(("owner", "split"), None), P(("owner", "split"))),
        out_specs=P(("owner", "split")),
        check_vma=False,
    )
```

```python
import functools
import jax
import jax.numpy as jnp
from jax import lax
from jax.experimental import pallas as pl
from jax.experimental.pallas import tpu as pltpu
from jax.sharding import PartitionSpec as P

CAP = 32
LANES = 128
META = 8
EMPTY = 262144.0
TILE = 512
PART = 512
PER_TILE = TILE // CAP
PER_ROW = LANES // CAP


def pack_kernel(emb_ref, code_ref, out_ref, target_ref, unit_ref):
    rows, width = emb_ref.shape
    owners = out_ref.shape[0]
    code = code_ref[...]
    cid = (code >> 16).astype(jnp.float32)
    column = jnp.transpose(jnp.broadcast_to(cid, (LANES, rows)))
    above = lax.broadcasted_iota(jnp.int32, (LANES, LANES), 0)
    here = lax.broadcasted_iota(jnp.int32, (LANES, LANES), 1)
    for j in range(rows // LANES):
        lanes = slice(j * LANES, (j + 1) * LANES)
        place = jnp.zeros((1, LANES), jnp.float32)
        for i in range(j + 1):
            same = column[i * LANES : (i + 1) * LANES] == cid[:, lanes]
            if i == j:
                same = same & (above < here)
            place += jnp.sum(jnp.where(same, 1.0, 0.0), axis=0, keepdims=True)
        target_ref[:, lanes] = (cid[:, lanes] * CAP + place).astype(jnp.int32)
    rank = (code & 65535) + 1
    high = jnp.broadcast_to((rank >> 8).astype(jnp.float32), (META // 2, rows))
    low = jnp.broadcast_to((rank & 255).astype(jnp.float32), (META // 2, rows))
    both = jnp.concatenate([high, low, jnp.zeros((LANES - META, rows), jnp.float32)], axis=0)
    unit_ref[:, width:] = jnp.transpose(both).astype(jnp.bfloat16)
    chunk = 128
    for r in range(rows // chunk):
        part = slice(r * chunk, (r + 1) * chunk)
        e = emb_ref[part, :].astype(jnp.float32)
        scale = lax.rsqrt(jnp.sum(e * e, axis=1, keepdims=True) + 1e-06)
        unit_ref[part, :width] = (e * scale).astype(jnp.bfloat16)
    target = target_ref[...]
    me = lax.axis_index("owner") % PER_ROW
    segment = lax.broadcasted_iota(jnp.int32, (META, LANES), 1) // CAP
    for step in range(owners // PER_TILE):
        block = slice(step * PER_TILE, (step + 1) * PER_TILE)
        slot = lax.broadcasted_iota(jnp.int32, (TILE, rows), 0)
        place = jnp.where(slot == target - step * TILE, 1.0, 0.0).astype(jnp.bfloat16)
        packed = jnp.dot(place, unit_ref[...], preferred_element_type=jnp.float32)
        for k in range(width // LANES):
            part = packed[:, k * LANES : (k + 1) * LANES].astype(jnp.bfloat16)
            out_ref[block, k * CAP : (k + 1) * CAP, :] = part.reshape(PER_TILE, CAP, LANES)
        ranks = jnp.transpose(packed[:, width:])[:META, :]
        for t in range(PER_TILE // PER_ROW):
            tile = ranks[:, t * LANES : (t + 1) * LANES]
            for q in range(PER_ROW):
                alone = jnp.where(segment == q, tile, 0.0)
                moved = pltpu.roll(alone, (me + PER_ROW - q) % PER_ROW * CAP, 1)
                out_ref[step * PER_TILE + t * PER_ROW + q, width // LANES * CAP :, :] = moved.astype(
                    jnp.bfloat16
                )


def pack(embeddings, code, owners):
    rows, width = embeddings.shape
    return pl.pallas_call(
        pack_kernel,
        out_shape=(
            jax.ShapeDtypeStruct((owners, width // LANES * CAP + META, LANES), jnp.bfloat16),
            jax.ShapeDtypeStruct((1, rows), jnp.int32),
        ),
        in_specs=[pl.BlockSpec(memory_space=pltpu.VMEM)] * 2,
        out_specs=(pl.BlockSpec(memory_space=pltpu.VMEM),) * 2,
        scratch_shapes=[pltpu.VMEM((rows, width + LANES), jnp.bfloat16)],
        compiler_params=pltpu.CompilerParams(vmem_limit_bytes=24 * 2**20),
        name="pack_rows",
    )(embeddings, code)


def rank_row(x_ref, group):
    meta = x_ref.shape[1] - META
    tiles = x_ref[group * PER_ROW : (group + 1) * PER_ROW, meta:, :].astype(jnp.float32)
    both = jnp.sum(tiles, axis=0)
    code = both[:1] * 256.0 + both[META // 2 : META // 2 + 1]
    return jnp.broadcast_to(jnp.where(code == 0.0, EMPTY, code), (8, LANES))


def as_column(row):
    return jnp.transpose(jnp.broadcast_to(row[:1], (LANES, LANES)))


def rows_of(x_ref, first, count):
    block = slice(first // CAP, (first + count) // CAP)
    columns = (x_ref.shape[1] - META) // CAP
    parts = [x_ref[block, k * CAP : (k + 1) * CAP, :].reshape(count, LANES) for k in range(columns)]
    return jnp.concatenate(parts, axis=1)


def compare(x, y, first, start, column_ref, row_ref, rows_ref, across):
    sims = lax.dot_general(x, y, (((1,), (1,)), ((), ())), preferred_element_type=jnp.float32)
    some = slice(first, first + x.shape[0])
    column = column_ref[some, :]
    best = rows_ref[some, :]
    for j in range(y.shape[0] // LANES):
        s = sims[:, j * LANES : (j + 1) * LANES]
        earlier = row_ref[:1, start + j * LANES : start + (j + 1) * LANES] < column
        best = jnp.maximum(best, jnp.where(earlier, s, -1.0))
        if across[j] is not None:
            later = jnp.where(earlier, -1.0, s)
            across[j] = jnp.maximum(across[j], jnp.max(later.reshape(-1, 8, LANES), axis=0))
    rows_ref[some, :] = best


def lowest():
    return jnp.full((8, LANES), -1.0, jnp.float32)


def own_kernel(x_ref, out_ref, column_ref, row_ref, rows_ref, columns_ref):
    count = x_ref.shape[0] * CAP
    rows_ref[...] = jnp.full(rows_ref.shape, -1.0, jnp.float32)
    for g in range(count // LANES):
        lanes = slice(g * LANES, (g + 1) * LANES)
        row = rank_row(x_ref, g)
        row_ref[:, lanes] = row
        column_ref[lanes, :] = as_column(row)
    per = TILE // LANES
    for start in range(0, count, TILE):
        y = rows_of(x_ref, start, TILE)
        across = [lowest() for _ in range(per)]
        for first in range(0, start, PART):
            x = rows_of(x_ref, first, PART)
            compare(x, y, first, start, column_ref, row_ref, rows_ref, across)
        half = per // 2
        x = rows_of(x_ref, start, TILE // 2)
        some = [None] * half + across[half:]
        compare(x, y, start, start, column_ref, row_ref, rows_ref, some)
        across[half:] = some[half:]
        middle = start + TILE // 2
        x = rows_of(x_ref, middle, TILE // 2)
        compare(x, x, middle, middle, column_ref, row_ref, rows_ref, [None] * half)
        for j in range(per):
            columns_ref[:, start + j * LANES : start + (j + 1) * LANES] = across[j]
    for g in range(count // LANES):
        a = slice(g * LANES, (g + 1) * LANES)
        best = jnp.max(jnp.transpose(rows_ref[a, :]), axis=0, keepdims=True)
        best = jnp.maximum(best, jnp.max(columns_ref[:, a], axis=0, keepdims=True))
        out_ref[:, a] = jnp.broadcast_to(best, (8, LANES))


def own_pairs(x, width):
    owners = x.shape[0]
    count = owners * CAP
    return pl.pallas_call(
        own_kernel,
        out_shape=jax.ShapeDtypeStruct((8, count), jnp.float32),
        in_specs=[pl.BlockSpec(memory_space=pltpu.VMEM)],
        out_specs=pl.BlockSpec(memory_space=pltpu.VMEM),
        scratch_shapes=[
            pltpu.VMEM((count, LANES), jnp.float32),
            pltpu.VMEM((8, count), jnp.float32),
            pltpu.VMEM((count, LANES), jnp.float32),
            pltpu.VMEM((8, count), jnp.float32),
        ],
        compiler_params=pltpu.CompilerParams(vmem_limit_bytes=24 * 2**20),
        cost_estimate=pl.CostEstimate(
            flops=count * (count + TILE) * width, bytes_accessed=2 * count * width, transcendentals=0
        ),
        name="own_pairs",
    )(x)


def cross(all_ref, some_ref, column_ref, row_ref, rows_ref, columns_ref):
    count = all_ref.shape[0] * CAP
    rows_ref[...] = jnp.full(rows_ref.shape, -1.0, jnp.float32)
    for g in range(count // LANES):
        lanes = slice(g * LANES, (g + 1) * LANES)
        column_ref[lanes, :] = as_column(rank_row(all_ref, g))
        row_ref[:, lanes] = rank_row(some_ref, g)
    for start in range(0, count, TILE):
        y = rows_of(some_ref, start, TILE)
        lanes = [slice(start + j * LANES, start + (j + 1) * LANES) for j in range(TILE // LANES)]
        across = [columns_ref[:, part] for part in lanes]
        for first in range(0, count, PART):
            x = rows_of(all_ref, first, PART)
            compare(x, y, first, start, column_ref, row_ref, rows_ref, across)
        for part, best in zip(lanes, across):
            columns_ref[:, part] = best


def first_kernel(x_ref, y_ref, rows_out, columns_out, column_ref, row_ref, rows_ref):
    core = lax.axis_index("split")
    half = y_ref.shape[0]
    columns_out[...] = jnp.full(columns_out.shape, -1.0, jnp.float32)

    @pl.when(core == 0)
    def _():
        cross(x_ref.at[:half], y_ref, column_ref, row_ref, rows_ref, columns_out)

    @pl.when(core != 0)
    def _():
        cross(y_ref, x_ref.at[half:], column_ref, row_ref, rows_ref, columns_out)

    for g in range(half * CAP // LANES):
        a = slice(g * LANES, (g + 1) * LANES)
        best = jnp.max(jnp.transpose(rows_ref[a, :]), axis=0, keepdims=True)
        rows_out[:, a] = jnp.broadcast_to(best, (8, LANES))


def second_kernel(
    x_ref, y_ref, z_ref, own_ref, first_ref, columns_in, out_ref, column_ref, row_ref, rows_ref, columns_ref
):
    core = lax.axis_index("split")
    half = y_ref.shape[0]
    columns_ref[...] = columns_in[...]

    @pl.when(core == 0)
    def _():
        cross(x_ref.at[half:], y_ref, column_ref, row_ref, rows_ref, columns_ref)

    @pl.when(core != 0)
    def _():
        cross(z_ref, x_ref.at[half:], column_ref, row_ref, rows_ref, columns_ref)

    parity = lax.broadcasted_iota(jnp.int32, (8, LANES), 0) % 2
    groups = half * CAP // LANES
    nothing = jnp.full((1, LANES), -1.0, jnp.float32)
    for g in range(2 * groups):
        a = slice(g * LANES, (g + 1) * LANES)
        b = slice(g % groups * LANES, (g % groups + 1) * LANES)
        if g < groups:
            from_all = first_ref[:1, b]
        else:
            from_all = jnp.max(jnp.transpose(rows_ref[b, :]), axis=0, keepdims=True)
        from_half = jnp.max(columns_ref[:, b], axis=0, keepdims=True)
        low, high = (from_half, nothing) if g < groups else (nothing, from_half)
        mine = jnp.maximum(own_ref[:1, a], jnp.where(core == 0, from_all, high))
        theirs = jnp.where(core == 0, low, from_all)
        out_ref[g * 8 : (g + 1) * 8, :] = jnp.where(
            parity == core, jnp.broadcast_to(mine, (8, LANES)), jnp.broadcast_to(theirs, (8, LANES))
        )


def cross_pairs(x, y, z, own, width):
    half = y.shape[0] * CAP
    cost = pl.CostEstimate(flops=2 * half * half * width, bytes_accessed=4 * half * width, transcendentals=0)
    vmem = pl.BlockSpec(memory_space=pltpu.VMEM)
    scratch = [
        pltpu.VMEM((half, LANES), jnp.float32),
        pltpu.VMEM((8, half), jnp.float32),
        pltpu.VMEM((half, LANES), jnp.float32),
    ]
    params = pltpu.CompilerParams(vmem_limit_bytes=24 * 2**20)
    first, columns = pl.pallas_call(
        first_kernel,
        out_shape=(jax.ShapeDtypeStruct((8, half), jnp.float32),) * 2,
        in_specs=[vmem] * 2,
        out_specs=(vmem,) * 2,
        scratch_shapes=scratch,
        compiler_params=params,
        cost_estimate=cost,
        name="cross_first",
    )(x, y)
    return pl.pallas_call(
        second_kernel,
        out_shape=jax.ShapeDtypeStruct((2 * half // LANES * 8, LANES), jnp.float32),
        in_specs=[vmem] * 6,
        out_specs=vmem,
        scratch_shapes=scratch + [pltpu.VMEM((8, half), jnp.float32)],
        compiler_params=params,
        cost_estimate=cost,
        name="cross_second",
    )(x, y, z, own, first, columns)


def pick_kernel(recv_ref, target_ref, out_ref):
    pairs = recv_ref.shape[0]
    owners = pairs // 2
    best = jnp.maximum(
        recv_ref[pl.ds(0, owners, stride=2), :], recv_ref[pl.ds(1, owners, stride=2), :]
    )
    target = target_ref[...]
    rows = target.shape[1]
    cid = target >> 5
    slot = (target & (CAP - 1)) + lax.axis_index("owner") % PER_ROW * CAP
    chosen = lax.broadcasted_iota(jnp.int32, (owners, rows), 0) == cid
    chosen = chosen.astype(jnp.float32).astype(jnp.bfloat16)
    total = jnp.zeros((LANES, rows), jnp.float32)
    rest = best
    for _ in range(3):
        piece = rest.astype(jnp.bfloat16)
        rest = rest - piece.astype(jnp.float32)
        total += lax.dot_general(
            piece, chosen, (((0,), (0,)), ((), ())), preferred_element_type=jnp.float32
        )
    mine = lax.broadcasted_iota(jnp.int32, (LANES, rows), 0) == slot
    out_ref[...] = jnp.sum(jnp.where(mine, total, 0.0), axis=0, keepdims=True)


def pick(recv, target):
    return pl.pallas_call(
        pick_kernel,
        out_shape=jax.ShapeDtypeStruct(target.shape, jnp.float32),
        in_specs=[pl.BlockSpec(memory_space=pltpu.VMEM)] * 2,
        out_specs=pl.BlockSpec(memory_space=pltpu.VMEM),
        compiler_params=pltpu.CompilerParams(vmem_limit_bytes=8 * 2**20),
        name="pick_results",
    )(recv, target)


def shards(embeddings, cluster, order):
    owners = lax.axis_size("owner")
    rows, width = embeddings.shape
    cid, rank = lax.optimization_barrier((cluster.reshape(1, rows), order.reshape(1, rows)))
    code = cid * 65536 + rank
    packed, target = pack(embeddings, code, owners)
    mine = lax.all_to_all(packed, "owner", split_axis=0, concat_axis=0, tiled=True)
    swap = [(0, 1), (1, 0)]
    half = owners // 2
    first = lax.ppermute(mine[:half], "split", swap)
    second = lax.ppermute(mine[half:], "split", swap)
    own = own_pairs(mine, width)
    best = cross_pairs(mine, first, second, own, width)
    returned = lax.all_to_all(best, ("owner", "split"), split_axis=0, concat_axis=0, tiled=True)
    return pick(returned, target).reshape(rows)


def solution(mesh):
    return jax.shard_map(
        shards,
        mesh=mesh,
        in_specs=(P(("owner", "split"), None), P(("owner", "split"), None), P(("owner", "split"))),
        out_specs=P(("owner", "split")),
        check_vma=False,
    )
```

```python
import functools
import jax
import jax.numpy as jnp
from jax import lax
from jax.experimental import pallas as pl
from jax.experimental.pallas import tpu as pltpu
from jax.sharding import PartitionSpec as P

CAP = 32
LANES = 128
META = 8
EMPTY = 262144.0
TILE = 512
PART = 512
PER_TILE = TILE // CAP
PER_ROW = LANES // CAP


def pack_kernel(emb_ref, code_ref, out_ref, target_ref, unit_ref, sorted_ref, counts_ref, counts_smem, sem):
    rows, width = emb_ref.shape
    owners = out_ref.shape[0]
    columns = width // LANES
    code = code_ref[...]
    cid = (code >> 16).astype(jnp.float32)
    column = jnp.transpose(jnp.broadcast_to(cid, (LANES, rows)))
    above = lax.broadcasted_iota(jnp.int32, (LANES, LANES), 0)
    here = lax.broadcasted_iota(jnp.int32, (LANES, LANES), 1)
    before = jnp.sum(jnp.where(column < here[:1].astype(jnp.float32), 1.0, 0.0), axis=0, keepdims=True)
    number = jnp.sum(jnp.where(column == here[:1].astype(jnp.float32), 1.0, 0.0), axis=0, keepdims=True)
    counts_ref[...] = jnp.zeros(counts_ref.shape, jnp.int32)
    counts_ref[0:1, :] = before.astype(jnp.int32)
    counts_ref[1:2, :] = number.astype(jnp.int32)
    copy = pltpu.make_async_copy(counts_ref, counts_smem, sem)
    copy.start()
    goals = []
    for j in range(rows // LANES):
        lanes = slice(j * LANES, (j + 1) * LANES)
        place = jnp.zeros((1, LANES), jnp.float32)
        lower = jnp.zeros((1, LANES), jnp.float32)
        for i in range(rows // LANES):
            other = column[i * LANES : (i + 1) * LANES]
            lower += jnp.sum(jnp.where(other < cid[:, lanes], 1.0, 0.0), axis=0, keepdims=True)
            if i <= j:
                same = other == cid[:, lanes]
                if i == j:
                    same = same & (above < here)
                place += jnp.sum(jnp.where(same, 1.0, 0.0), axis=0, keepdims=True)
        target_ref[:, lanes] = (cid[:, lanes] * CAP + place).astype(jnp.int32)
        goals.append((lower + place).astype(jnp.int32))
    rank = (code & 65535) + 1
    high = jnp.broadcast_to((rank >> 8).astype(jnp.float32), (META // 2, rows))
    low = jnp.broadcast_to((rank & 255).astype(jnp.float32), (META // 2, rows))
    both = jnp.concatenate([high, low, jnp.zeros((LANES - META, rows), jnp.float32)], axis=0)
    unit_ref[:, width:] = jnp.transpose(both).astype(jnp.bfloat16)
    chunk = 128
    for r in range(rows // chunk):
        part = slice(r * chunk, (r + 1) * chunk)
        e = emb_ref[part, :].astype(jnp.float32)
        scale = lax.rsqrt(jnp.sum(e * e, axis=1, keepdims=True) + 1e-06)
        unit_ref[part, :width] = (e * scale).astype(jnp.bfloat16)
    slot = lax.broadcasted_iota(jnp.int32, (rows, rows), 0)
    place = jnp.where(slot == jnp.concatenate(goals, axis=1), 1.0, 0.0).astype(jnp.bfloat16)
    ordered = jnp.dot(place, unit_ref[...], preferred_element_type=jnp.float32)
    for k in range(columns + 1):
        sorted_ref[k, :rows, :] = ordered[:, k * LANES : (k + 1) * LANES]
        sorted_ref[k, rows:, :] = jnp.zeros((CAP, LANES), jnp.float32)
    copy.wait()
    me = lax.axis_index("owner") % PER_ROW
    segment = lax.broadcasted_iota(jnp.int32, (META, LANES), 1) // CAP
    line = lax.broadcasted_iota(jnp.int32, (CAP, LANES), 0)
    for group in range(owners // PER_ROW):
        ranks = []
        for q in range(PER_ROW):
            c = group * PER_ROW + q
            some = pl.ds(counts_smem[0, c], CAP)
            for k in range(columns):
                out_ref[c, k * CAP : (k + 1) * CAP, :] = sorted_ref[k, some, :].astype(jnp.bfloat16)
            ranks.append(jnp.where(line < counts_smem[1, c], sorted_ref[columns, some, :], 0.0))
        tile = jnp.transpose(jnp.concatenate(ranks, axis=0))[:META, :]
        for q in range(PER_ROW):
            alone = jnp.where(segment == q, tile, 0.0)
            moved = pltpu.roll(alone, (me + PER_ROW - q) % PER_ROW * CAP, 1)
            out_ref[group * PER_ROW + q, columns * CAP :, :] = moved.astype(jnp.bfloat16)


def pack(embeddings, code, owners):
    rows, width = embeddings.shape
    return pl.pallas_call(
        pack_kernel,
        out_shape=(
            jax.ShapeDtypeStruct((owners, width // LANES * CAP + META, LANES), jnp.bfloat16),
            jax.ShapeDtypeStruct((1, rows), jnp.int32),
        ),
        in_specs=[pl.BlockSpec(memory_space=pltpu.VMEM)] * 2,
        out_specs=(pl.BlockSpec(memory_space=pltpu.VMEM),) * 2,
        scratch_shapes=[
            pltpu.VMEM((rows, width + LANES), jnp.bfloat16),
            pltpu.VMEM((width // LANES + 1, rows + CAP, LANES), jnp.float32),
            pltpu.VMEM((8, LANES), jnp.int32),
            pltpu.SMEM((8, LANES), jnp.int32),
            pltpu.SemaphoreType.DMA(()),
        ],
        compiler_params=pltpu.CompilerParams(vmem_limit_bytes=24 * 2**20),
        name="pack_rows",
    )(embeddings, code)


def rank_row(x_ref, group):
    meta = x_ref.shape[1] - META
    tiles = x_ref[group * PER_ROW : (group + 1) * PER_ROW, meta:, :].astype(jnp.float32)
    both = jnp.sum(tiles, axis=0)
    code = both[:1] * 256.0 + both[META // 2 : META // 2 + 1]
    return jnp.broadcast_to(jnp.where(code == 0.0, EMPTY, code), (8, LANES))


def as_column(row):
    return jnp.transpose(jnp.broadcast_to(row[:1], (LANES, LANES)))


def rows_of(x_ref, first, count):
    block = slice(first // CAP, (first + count) // CAP)
    columns = (x_ref.shape[1] - META) // CAP
    parts = [x_ref[block, k * CAP : (k + 1) * CAP, :].reshape(count, LANES) for k in range(columns)]
    return jnp.concatenate(parts, axis=1)


def compare(x, y, first, start, column_ref, row_ref, rows_ref, across):
    sims = lax.dot_general(x, y, (((1,), (1,)), ((), ())), preferred_element_type=jnp.float32)
    some = slice(first, first + x.shape[0])
    column = column_ref[some, :]
    best = rows_ref[some, :]
    for j in range(y.shape[0] // LANES):
        s = sims[:, j * LANES : (j + 1) * LANES]
        earlier = row_ref[:1, start + j * LANES : start + (j + 1) * LANES] < column
        best = jnp.maximum(best, jnp.where(earlier, s, -1.0))
        if across[j] is not None:
            later = jnp.where(earlier, -1.0, s)
            across[j] = jnp.maximum(across[j], jnp.max(later.reshape(-1, 8, LANES), axis=0))
    rows_ref[some, :] = best


def lowest():
    return jnp.full((8, LANES), -1.0, jnp.float32)


def own_kernel(x_ref, out_ref, column_ref, row_ref, rows_ref, columns_ref):
    count = x_ref.shape[0] * CAP
    rows_ref[...] = jnp.full(rows_ref.shape, -1.0, jnp.float32)
    for g in range(count // LANES):
        lanes = slice(g * LANES, (g + 1) * LANES)
        row = rank_row(x_ref, g)
        row_ref[:, lanes] = row
        column_ref[lanes, :] = as_column(row)
    per = TILE // LANES
    for start in range(0, count, TILE):
        y = rows_of(x_ref, start, TILE)
        across = [lowest() for _ in range(per)]
        for first in range(0, start, PART):
            x = rows_of(x_ref, first, PART)
            compare(x, y, first, start, column_ref, row_ref, rows_ref, across)
        half = per // 2
        x = rows_of(x_ref, start, TILE // 2)
        some = [None] * half + across[half:]
        compare(x, y, start, start, column_ref, row_ref, rows_ref, some)
        across[half:] = some[half:]
        middle = start + TILE // 2
        x = rows_of(x_ref, middle, TILE // 2)
        compare(x, x, middle, middle, column_ref, row_ref, rows_ref, [None] * half)
        for j in range(per):
            columns_ref[:, start + j * LANES : start + (j + 1) * LANES] = across[j]
    for g in range(count // LANES):
        a = slice(g * LANES, (g + 1) * LANES)
        best = jnp.max(jnp.transpose(rows_ref[a, :]), axis=0, keepdims=True)
        best = jnp.maximum(best, jnp.max(columns_ref[:, a], axis=0, keepdims=True))
        out_ref[:, a] = jnp.broadcast_to(best, (8, LANES))


def own_pairs(x, width):
    owners = x.shape[0]
    count = owners * CAP
    return pl.pallas_call(
        own_kernel,
        out_shape=jax.ShapeDtypeStruct((8, count), jnp.float32),
        in_specs=[pl.BlockSpec(memory_space=pltpu.VMEM)],
        out_specs=pl.BlockSpec(memory_space=pltpu.VMEM),
        scratch_shapes=[
            pltpu.VMEM((count, LANES), jnp.float32),
            pltpu.VMEM((8, count), jnp.float32),
            pltpu.VMEM((count, LANES), jnp.float32),
            pltpu.VMEM((8, count), jnp.float32),
        ],
        compiler_params=pltpu.CompilerParams(vmem_limit_bytes=24 * 2**20),
        cost_estimate=pl.CostEstimate(
            flops=count * (count + TILE) * width, bytes_accessed=2 * count * width, transcendentals=0
        ),
        name="own_pairs",
    )(x)


def cross(all_ref, some_ref, column_ref, row_ref, rows_ref, columns_ref):
    count = all_ref.shape[0] * CAP
    rows_ref[...] = jnp.full(rows_ref.shape, -1.0, jnp.float32)
    for g in range(count // LANES):
        lanes = slice(g * LANES, (g + 1) * LANES)
        column_ref[lanes, :] = as_column(rank_row(all_ref, g))
        row_ref[:, lanes] = rank_row(some_ref, g)
    for start in range(0, count, TILE):
        y = rows_of(some_ref, start, TILE)
        lanes = [slice(start + j * LANES, start + (j + 1) * LANES) for j in range(TILE // LANES)]
        across = [columns_ref[:, part] for part in lanes]
        for first in range(0, count, PART):
            x = rows_of(all_ref, first, PART)
            compare(x, y, first, start, column_ref, row_ref, rows_ref, across)
        for part, best in zip(lanes, across):
            columns_ref[:, part] = best


def first_kernel(x_ref, y_ref, rows_out, columns_out, column_ref, row_ref, rows_ref):
    core = lax.axis_index("split")
    half = y_ref.shape[0]
    columns_out[...] = jnp.full(columns_out.shape, -1.0, jnp.float32)

    @pl.when(core == 0)
    def _():
        cross(x_ref.at[:half], y_ref, column_ref, row_ref, rows_ref, columns_out)

    @pl.when(core != 0)
    def _():
        cross(y_ref, x_ref.at[half:], column_ref, row_ref, rows_ref, columns_out)

    for g in range(half * CAP // LANES):
        a = slice(g * LANES, (g + 1) * LANES)
        best = jnp.max(jnp.transpose(rows_ref[a, :]), axis=0, keepdims=True)
        rows_out[:, a] = jnp.broadcast_to(best, (8, LANES))


def second_kernel(
    x_ref, y_ref, z_ref, own_ref, first_ref, columns_in, out_ref, column_ref, row_ref, rows_ref, columns_ref
):
    core = lax.axis_index("split")
    half = y_ref.shape[0]
    columns_ref[...] = columns_in[...]

    @pl.when(core == 0)
    def _():
        cross(x_ref.at[half:], y_ref, column_ref, row_ref, rows_ref, columns_ref)

    @pl.when(core != 0)
    def _():
        cross(z_ref, x_ref.at[half:], column_ref, row_ref, rows_ref, columns_ref)

    parity = lax.broadcasted_iota(jnp.int32, (8, LANES), 0) % 2
    groups = half * CAP // LANES
    nothing = jnp.full((1, LANES), -1.0, jnp.float32)
    for g in range(2 * groups):
        a = slice(g * LANES, (g + 1) * LANES)
        b = slice(g % groups * LANES, (g % groups + 1) * LANES)
        if g < groups:
            from_all = first_ref[:1, b]
        else:
            from_all = jnp.max(jnp.transpose(rows_ref[b, :]), axis=0, keepdims=True)
        from_half = jnp.max(columns_ref[:, b], axis=0, keepdims=True)
        low, high = (from_half, nothing) if g < groups else (nothing, from_half)
        mine = jnp.maximum(own_ref[:1, a], jnp.where(core == 0, from_all, high))
        theirs = jnp.where(core == 0, low, from_all)
        out_ref[g * 8 : (g + 1) * 8, :] = jnp.where(
            parity == core, jnp.broadcast_to(mine, (8, LANES)), jnp.broadcast_to(theirs, (8, LANES))
        )


def cross_pairs(x, y, z, own, width):
    half = y.shape[0] * CAP
    cost = pl.CostEstimate(flops=2 * half * half * width, bytes_accessed=4 * half * width, transcendentals=0)
    vmem = pl.BlockSpec(memory_space=pltpu.VMEM)
    scratch = [
        pltpu.VMEM((half, LANES), jnp.float32),
        pltpu.VMEM((8, half), jnp.float32),
        pltpu.VMEM((half, LANES), jnp.float32),
    ]
    params = pltpu.CompilerParams(vmem_limit_bytes=24 * 2**20)
    first, columns = pl.pallas_call(
        first_kernel,
        out_shape=(jax.ShapeDtypeStruct((8, half), jnp.float32),) * 2,
        in_specs=[vmem] * 2,
        out_specs=(vmem,) * 2,
        scratch_shapes=scratch,
        compiler_params=params,
        cost_estimate=cost,
        name="cross_first",
    )(x, y)
    return pl.pallas_call(
        second_kernel,
        out_shape=jax.ShapeDtypeStruct((2 * half // LANES * 8, LANES), jnp.float32),
        in_specs=[vmem] * 6,
        out_specs=vmem,
        scratch_shapes=scratch + [pltpu.VMEM((8, half), jnp.float32)],
        compiler_params=params,
        cost_estimate=cost,
        name="cross_second",
    )(x, y, z, own, first, columns)


def pick_kernel(recv_ref, target_ref, out_ref):
    pairs = recv_ref.shape[0]
    owners = pairs // 2
    best = jnp.maximum(
        recv_ref[pl.ds(0, owners, stride=2), :], recv_ref[pl.ds(1, owners, stride=2), :]
    )
    target = target_ref[...]
    rows = target.shape[1]
    cid = target >> 5
    slot = (target & (CAP - 1)) + lax.axis_index("owner") % PER_ROW * CAP
    chosen = lax.broadcasted_iota(jnp.int32, (owners, rows), 0) == cid
    chosen = chosen.astype(jnp.float32).astype(jnp.bfloat16)
    total = jnp.zeros((LANES, rows), jnp.float32)
    rest = best
    for _ in range(3):
        piece = rest.astype(jnp.bfloat16)
        rest = rest - piece.astype(jnp.float32)
        total += lax.dot_general(
            piece, chosen, (((0,), (0,)), ((), ())), preferred_element_type=jnp.float32
        )
    mine = lax.broadcasted_iota(jnp.int32, (LANES, rows), 0) == slot
    out_ref[...] = jnp.sum(jnp.where(mine, total, 0.0), axis=0, keepdims=True)


def pick(recv, target):
    return pl.pallas_call(
        pick_kernel,
        out_shape=jax.ShapeDtypeStruct(target.shape, jnp.float32),
        in_specs=[pl.BlockSpec(memory_space=pltpu.VMEM)] * 2,
        out_specs=pl.BlockSpec(memory_space=pltpu.VMEM),
        compiler_params=pltpu.CompilerParams(vmem_limit_bytes=8 * 2**20),
        name="pick_results",
    )(recv, target)


def shards(embeddings, cluster, order):
    owners = lax.axis_size("owner")
    rows, width = embeddings.shape
    cid, rank = lax.optimization_barrier((cluster.reshape(1, rows), order.reshape(1, rows)))
    code = cid * 65536 + rank
    packed, target = pack(embeddings, code, owners)
    mine = lax.all_to_all(packed, "owner", split_axis=0, concat_axis=0, tiled=True)
    swap = [(0, 1), (1, 0)]
    half = owners // 2
    first = lax.ppermute(mine[:half], "split", swap)
    second = lax.ppermute(mine[half:], "split", swap)
    own = own_pairs(mine, width)
    best = cross_pairs(mine, first, second, own, width)
    returned = lax.all_to_all(best, ("owner", "split"), split_axis=0, concat_axis=0, tiled=True)
    return pick(returned, target).reshape(rows)


def solution(mesh):
    return jax.shard_map(
        shards,
        mesh=mesh,
        in_specs=(P(("owner", "split"), None), P(("owner", "split"), None), P(("owner", "split"))),
        out_specs=P(("owner", "split")),
        check_vma=False,
    )
```

```python
import functools
import jax
import jax.numpy as jnp
from jax import lax
from jax.experimental import pallas as pl
from jax.experimental.pallas import tpu as pltpu
from jax.sharding import PartitionSpec as P

CAP = 32
LANES = 128
META = 16
EMPTY = 262144.0
TILE = 512
PART = 512
PER_TILE = TILE // CAP
PER_ROW = LANES // CAP


def pack_kernel(emb_ref, code_ref, out_ref, target_ref, unit_ref, sorted_ref, counts_ref, counts_smem, sem):
    rows, width = emb_ref.shape
    owners = out_ref.shape[0]
    columns = width // LANES
    code = code_ref[...]
    cid = (code >> 16).astype(jnp.float32)
    column = jnp.transpose(jnp.broadcast_to(cid, (LANES, rows)))
    above = lax.broadcasted_iota(jnp.int32, (LANES, LANES), 0)
    here = lax.broadcasted_iota(jnp.int32, (LANES, LANES), 1)
    before = jnp.sum(jnp.where(column < here[:1].astype(jnp.float32), 1.0, 0.0), axis=0, keepdims=True)
    number = jnp.sum(jnp.where(column == here[:1].astype(jnp.float32), 1.0, 0.0), axis=0, keepdims=True)
    counts_ref[...] = jnp.zeros(counts_ref.shape, jnp.int32)
    counts_ref[0:1, :] = before.astype(jnp.int32)
    counts_ref[1:2, :] = number.astype(jnp.int32)
    copy = pltpu.make_async_copy(counts_ref, counts_smem, sem)
    copy.start()
    goals = []
    for j in range(rows // LANES):
        lanes = slice(j * LANES, (j + 1) * LANES)
        place = jnp.zeros((1, LANES), jnp.float32)
        lower = jnp.zeros((1, LANES), jnp.float32)
        for i in range(rows // LANES):
            other = column[i * LANES : (i + 1) * LANES]
            lower += jnp.sum(jnp.where(other < cid[:, lanes], 1.0, 0.0), axis=0, keepdims=True)
            if i <= j:
                same = other == cid[:, lanes]
                if i == j:
                    same = same & (above < here)
                place += jnp.sum(jnp.where(same, 1.0, 0.0), axis=0, keepdims=True)
        target_ref[:, lanes] = (cid[:, lanes] * CAP + place).astype(jnp.int32)
        goals.append((lower + place).astype(jnp.int32))
    rank = (code & 65535) + 1
    high = jnp.broadcast_to((rank >> 8).astype(jnp.float32), (META // 2, rows))
    low = jnp.broadcast_to((rank & 255).astype(jnp.float32), (META // 2, rows))
    both = jnp.concatenate([high, low, jnp.zeros((LANES - META, rows), jnp.float32)], axis=0)
    unit_ref[:, width:] = jnp.transpose(both).astype(jnp.bfloat16)
    chunk = 128
    for r in range(rows // chunk):
        part = slice(r * chunk, (r + 1) * chunk)
        e = emb_ref[part, :].astype(jnp.float32)
        scale = lax.rsqrt(jnp.sum(e * e, axis=1, keepdims=True) + 1e-06)
        unit_ref[part, :width] = (e * scale).astype(jnp.bfloat16)
    slot = lax.broadcasted_iota(jnp.int32, (rows, rows), 0)
    place = jnp.where(slot == jnp.concatenate(goals, axis=1), 1.0, 0.0).astype(jnp.bfloat16)
    ordered = jnp.dot(place, unit_ref[...], preferred_element_type=jnp.float32)
    for k in range(columns + 1):
        sorted_ref[k, :rows, :] = ordered[:, k * LANES : (k + 1) * LANES]
        sorted_ref[k, rows:, :] = jnp.zeros((CAP, LANES), jnp.float32)
    copy.wait()
    me = lax.axis_index("owner") % PER_ROW
    segment = lax.broadcasted_iota(jnp.int32, (META, LANES), 1) // CAP
    line = lax.broadcasted_iota(jnp.int32, (CAP, LANES), 0)
    for group in range(owners // PER_ROW):
        ranks = []
        for q in range(PER_ROW):
            c = group * PER_ROW + q
            some = pl.ds(counts_smem[0, c], CAP)
            for k in range(columns):
                out_ref[c, k * CAP : (k + 1) * CAP, :] = sorted_ref[k, some, :].astype(jnp.bfloat16)
            ranks.append(jnp.where(line < counts_smem[1, c], sorted_ref[columns, some, :], 0.0))
        tile = jnp.transpose(jnp.concatenate(ranks, axis=0))[:META, :]
        for q in range(PER_ROW):
            alone = jnp.where(segment == q, tile, 0.0)
            moved = pltpu.roll(alone, (me + PER_ROW - q) % PER_ROW * CAP, 1)
            out_ref[group * PER_ROW + q, columns * CAP :, :] = moved.astype(jnp.bfloat16)


def pack(embeddings, code, owners):
    rows, width = embeddings.shape
    return pl.pallas_call(
        pack_kernel,
        out_shape=(
            jax.ShapeDtypeStruct((owners, width // LANES * CAP + META, LANES), jnp.bfloat16),
            jax.ShapeDtypeStruct((1, rows), jnp.int32),
        ),
        in_specs=[pl.BlockSpec(memory_space=pltpu.VMEM)] * 2,
        out_specs=(pl.BlockSpec(memory_space=pltpu.VMEM),) * 2,
        scratch_shapes=[
            pltpu.VMEM((rows, width + LANES), jnp.bfloat16),
            pltpu.VMEM((width // LANES + 1, rows + CAP, LANES), jnp.float32),
            pltpu.VMEM((8, LANES), jnp.int32),
            pltpu.SMEM((8, LANES), jnp.int32),
            pltpu.SemaphoreType.DMA(()),
        ],
        compiler_params=pltpu.CompilerParams(vmem_limit_bytes=24 * 2**20),
        name="pack_rows",
    )(embeddings, code)


def rank_row(x_ref, group):
    meta = x_ref.shape[1] - META
    tiles = x_ref[group * PER_ROW : (group + 1) * PER_ROW, meta:, :].astype(jnp.float32)
    both = jnp.sum(tiles, axis=0)
    code = both[:1] * 256.0 + both[META // 2 : META // 2 + 1]
    return jnp.broadcast_to(jnp.where(code == 0.0, EMPTY, code), (8, LANES))


def as_column(row):
    return jnp.transpose(jnp.broadcast_to(row[:1], (LANES, LANES)))


def rows_of(x_ref, first, count):
    block = slice(first // CAP, (first + count) // CAP)
    columns = (x_ref.shape[1] - META) // CAP
    parts = [x_ref[block, k * CAP : (k + 1) * CAP, :].reshape(count, LANES) for k in range(columns)]
    return jnp.concatenate(parts, axis=1)


def compare(x, y, first, start, column_ref, row_ref, rows_ref, across):
    sims = lax.dot_general(x, y, (((1,), (1,)), ((), ())), preferred_element_type=jnp.float32)
    some = slice(first, first + x.shape[0])
    column = column_ref[some, :]
    best = rows_ref[some, :]
    for j in range(y.shape[0] // LANES):
        s = sims[:, j * LANES : (j + 1) * LANES]
        earlier = row_ref[:1, start + j * LANES : start + (j + 1) * LANES] < column
        best = jnp.maximum(best, jnp.where(earlier, s, -1.0))
        if across[j] is not None:
            later = jnp.where(earlier, -1.0, s)
            across[j] = jnp.maximum(across[j], jnp.max(later.reshape(-1, 8, LANES), axis=0))
    rows_ref[some, :] = best


def lowest():
    return jnp.full((8, LANES), -1.0, jnp.float32)


def own_kernel(x_ref, out_ref, column_ref, row_ref, rows_ref, columns_ref):
    count = x_ref.shape[0] * CAP
    rows_ref[...] = jnp.full(rows_ref.shape, -1.0, jnp.float32)
    for g in range(count // LANES):
        lanes = slice(g * LANES, (g + 1) * LANES)
        row = rank_row(x_ref, g)
        row_ref[:, lanes] = row
        column_ref[lanes, :] = as_column(row)
    per = TILE // LANES
    for start in range(0, count, TILE):
        y = rows_of(x_ref, start, TILE)
        across = [lowest() for _ in range(per)]
        for first in range(0, start, PART):
            x = rows_of(x_ref, first, PART)
            compare(x, y, first, start, column_ref, row_ref, rows_ref, across)
        half = per // 2
        x = rows_of(x_ref, start, TILE // 2)
        some = [None] * half + across[half:]
        compare(x, y, start, start, column_ref, row_ref, rows_ref, some)
        across[half:] = some[half:]
        middle = start + TILE // 2
        x = rows_of(x_ref, middle, TILE // 2)
        compare(x, x, middle, middle, column_ref, row_ref, rows_ref, [None] * half)
        for j in range(per):
            columns_ref[:, start + j * LANES : start + (j + 1) * LANES] = across[j]
    for g in range(count // LANES):
        a = slice(g * LANES, (g + 1) * LANES)
        best = jnp.max(jnp.transpose(rows_ref[a, :]), axis=0, keepdims=True)
        best = jnp.maximum(best, jnp.max(columns_ref[:, a], axis=0, keepdims=True))
        out_ref[:, a] = jnp.broadcast_to(best, (8, LANES))


def own_pairs(x, width):
    owners = x.shape[0]
    count = owners * CAP
    return pl.pallas_call(
        own_kernel,
        out_shape=jax.ShapeDtypeStruct((8, count), jnp.float32),
        in_specs=[pl.BlockSpec(memory_space=pltpu.VMEM)],
        out_specs=pl.BlockSpec(memory_space=pltpu.VMEM),
        scratch_shapes=[
            pltpu.VMEM((count, LANES), jnp.float32),
            pltpu.VMEM((8, count), jnp.float32),
            pltpu.VMEM((count, LANES), jnp.float32),
            pltpu.VMEM((8, count), jnp.float32),
        ],
        compiler_params=pltpu.CompilerParams(vmem_limit_bytes=24 * 2**20),
        cost_estimate=pl.CostEstimate(
            flops=count * (count + TILE) * width, bytes_accessed=2 * count * width, transcendentals=0
        ),
        name="own_pairs",
    )(x)


def cross(all_ref, some_ref, column_ref, row_ref, rows_ref, columns_ref):
    count = all_ref.shape[0] * CAP
    rows_ref[...] = jnp.full(rows_ref.shape, -1.0, jnp.float32)
    for g in range(count // LANES):
        lanes = slice(g * LANES, (g + 1) * LANES)
        column_ref[lanes, :] = as_column(rank_row(all_ref, g))
        row_ref[:, lanes] = rank_row(some_ref, g)
    for start in range(0, count, TILE):
        y = rows_of(some_ref, start, TILE)
        lanes = [slice(start + j * LANES, start + (j + 1) * LANES) for j in range(TILE // LANES)]
        across = [columns_ref[:, part] for part in lanes]
        for first in range(0, count, PART):
            x = rows_of(all_ref, first, PART)
            compare(x, y, first, start, column_ref, row_ref, rows_ref, across)
        for part, best in zip(lanes, across):
            columns_ref[:, part] = best


def first_kernel(x_ref, y_ref, rows_out, columns_out, column_ref, row_ref, rows_ref):
    core = lax.axis_index("split")
    half = y_ref.shape[0]
    columns_out[...] = jnp.full(columns_out.shape, -1.0, jnp.float32)

    @pl.when(core == 0)
    def _():
        cross(x_ref.at[:half], y_ref, column_ref, row_ref, rows_ref, columns_out)

    @pl.when(core != 0)
    def _():
        cross(y_ref, x_ref.at[half:], column_ref, row_ref, rows_ref, columns_out)

    for g in range(half * CAP // LANES):
        a = slice(g * LANES, (g + 1) * LANES)
        best = jnp.max(jnp.transpose(rows_ref[a, :]), axis=0, keepdims=True)
        rows_out[:, a] = jnp.broadcast_to(best, (8, LANES))


def second_kernel(
    x_ref, y_ref, z_ref, own_ref, first_ref, columns_in, out_ref, column_ref, row_ref, rows_ref, columns_ref
):
    core = lax.axis_index("split")
    half = y_ref.shape[0]
    columns_ref[...] = columns_in[...]

    @pl.when(core == 0)
    def _():
        cross(x_ref.at[half:], y_ref, column_ref, row_ref, rows_ref, columns_ref)

    @pl.when(core != 0)
    def _():
        cross(z_ref, x_ref.at[half:], column_ref, row_ref, rows_ref, columns_ref)

    parity = lax.broadcasted_iota(jnp.int32, (8, LANES), 0) % 2
    groups = half * CAP // LANES
    nothing = jnp.full((1, LANES), -1.0, jnp.float32)
    for g in range(2 * groups):
        a = slice(g * LANES, (g + 1) * LANES)
        b = slice(g % groups * LANES, (g % groups + 1) * LANES)
        if g < groups:
            from_all = first_ref[:1, b]
        else:
            from_all = jnp.max(jnp.transpose(rows_ref[b, :]), axis=0, keepdims=True)
        from_half = jnp.max(columns_ref[:, b], axis=0, keepdims=True)
        low, high = (from_half, nothing) if g < groups else (nothing, from_half)
        mine = jnp.maximum(own_ref[:1, a], jnp.where(core == 0, from_all, high))
        theirs = jnp.where(core == 0, low, from_all)
        out_ref[g * 8 : (g + 1) * 8, :] = jnp.where(
            parity == core, jnp.broadcast_to(mine, (8, LANES)), jnp.broadcast_to(theirs, (8, LANES))
        )


def cross_pairs(x, y, z, own, width):
    half = y.shape[0] * CAP
    cost = pl.CostEstimate(flops=2 * half * half * width, bytes_accessed=4 * half * width, transcendentals=0)
    vmem = pl.BlockSpec(memory_space=pltpu.VMEM)
    scratch = [
        pltpu.VMEM((half, LANES), jnp.float32),
        pltpu.VMEM((8, half), jnp.float32),
        pltpu.VMEM((half, LANES), jnp.float32),
    ]
    params = pltpu.CompilerParams(vmem_limit_bytes=24 * 2**20)
    first, columns = pl.pallas_call(
        first_kernel,
        out_shape=(jax.ShapeDtypeStruct((8, half), jnp.float32),) * 2,
        in_specs=[vmem] * 2,
        out_specs=(vmem,) * 2,
        scratch_shapes=scratch,
        compiler_params=params,
        cost_estimate=cost,
        name="cross_first",
    )(x, y)
    return pl.pallas_call(
        second_kernel,
        out_shape=jax.ShapeDtypeStruct((2 * half // LANES * 8, LANES), jnp.float32),
        in_specs=[vmem] * 6,
        out_specs=vmem,
        scratch_shapes=scratch + [pltpu.VMEM((8, half), jnp.float32)],
        compiler_params=params,
        cost_estimate=cost,
        name="cross_second",
    )(x, y, z, own, first, columns)


def pick_kernel(recv_ref, target_ref, out_ref):
    pairs = recv_ref.shape[0]
    owners = pairs // 2
    best = jnp.maximum(
        recv_ref[pl.ds(0, owners, stride=2), :], recv_ref[pl.ds(1, owners, stride=2), :]
    )
    target = target_ref[...]
    rows = target.shape[1]
    cid = target >> 5
    slot = (target & (CAP - 1)) + lax.axis_index("owner") % PER_ROW * CAP
    chosen = lax.broadcasted_iota(jnp.int32, (owners, rows), 0) == cid
    chosen = chosen.astype(jnp.float32).astype(jnp.bfloat16)
    total = jnp.zeros((LANES, rows), jnp.float32)
    rest = best
    for _ in range(3):
        piece = rest.astype(jnp.bfloat16)
        rest = rest - piece.astype(jnp.float32)
        total += lax.dot_general(
            piece, chosen, (((0,), (0,)), ((), ())), preferred_element_type=jnp.float32
        )
    mine = lax.broadcasted_iota(jnp.int32, (LANES, rows), 0) == slot
    out_ref[...] = jnp.sum(jnp.where(mine, total, 0.0), axis=0, keepdims=True)


def pick(recv, target):
    return pl.pallas_call(
        pick_kernel,
        out_shape=jax.ShapeDtypeStruct(target.shape, jnp.float32),
        in_specs=[pl.BlockSpec(memory_space=pltpu.VMEM)] * 2,
        out_specs=pl.BlockSpec(memory_space=pltpu.VMEM),
        compiler_params=pltpu.CompilerParams(vmem_limit_bytes=8 * 2**20),
        name="pick_results",
    )(recv, target)


def shards(embeddings, cluster, order):
    owners = lax.axis_size("owner")
    rows, width = embeddings.shape
    cid, rank = lax.optimization_barrier((cluster.reshape(1, rows), order.reshape(1, rows)))
    code = cid * 65536 + rank
    packed, target = pack(embeddings, code, owners)
    mine = lax.all_to_all(packed, "owner", split_axis=0, concat_axis=0, tiled=True)
    swap = [(0, 1), (1, 0)]
    half = owners // 2
    first = lax.ppermute(mine[:half], "split", swap)
    second = lax.ppermute(mine[half:], "split", swap)
    own = own_pairs(mine, width)
    best = cross_pairs(mine, first, second, own, width)
    returned = lax.all_to_all(best, ("owner", "split"), split_axis=0, concat_axis=0, tiled=True)
    return pick(returned, target).reshape(rows)


def solution(mesh):
    return jax.shard_map(
        shards,
        mesh=mesh,
        in_specs=(P(("owner", "split"), None), P(("owner", "split"), None), P(("owner", "split"))),
        out_specs=P(("owner", "split")),
        check_vma=False,
    )
```

```python
import functools
import jax
import jax.numpy as jnp
from jax import lax
from jax.experimental import pallas as pl
from jax.experimental.pallas import tpu as pltpu
from jax.sharding import PartitionSpec as P

CAP = 32
LANES = 128
META = 8
EMPTY = 262144.0
TILE = 512
PART = 512
PER_TILE = TILE // CAP
PER_ROW = LANES // CAP


def pack_kernel(emb_ref, code_ref, out_ref, target_ref, unit_ref, sorted_ref, counts_ref, counts_smem, sem):
    rows, width = emb_ref.shape
    owners = out_ref.shape[0]
    columns = width // LANES
    code = code_ref[...]
    cid = (code >> 16).astype(jnp.float32)
    column = jnp.transpose(jnp.broadcast_to(cid, (LANES, rows)))
    above = lax.broadcasted_iota(jnp.int32, (LANES, LANES), 0)
    here = lax.broadcasted_iota(jnp.int32, (LANES, LANES), 1)
    before = jnp.sum(jnp.where(column < here[:1].astype(jnp.float32), 1.0, 0.0), axis=0, keepdims=True)
    number = jnp.sum(jnp.where(column == here[:1].astype(jnp.float32), 1.0, 0.0), axis=0, keepdims=True)
    counts_ref[...] = jnp.zeros(counts_ref.shape, jnp.int32)
    counts_ref[0:1, :] = before.astype(jnp.int32)
    counts_ref[1:2, :] = number.astype(jnp.int32)
    copy = pltpu.make_async_copy(counts_ref, counts_smem, sem)
    copy.start()
    goals = []
    for j in range(rows // LANES):
        lanes = slice(j * LANES, (j + 1) * LANES)
        place = jnp.zeros((1, LANES), jnp.float32)
        lower = jnp.zeros((1, LANES), jnp.float32)
        for i in range(rows // LANES):
            other = column[i * LANES : (i + 1) * LANES]
            lower += jnp.sum(jnp.where(other < cid[:, lanes], 1.0, 0.0), axis=0, keepdims=True)
            if i <= j:
                same = other == cid[:, lanes]
                if i == j:
                    same = same & (above < here)
                place += jnp.sum(jnp.where(same, 1.0, 0.0), axis=0, keepdims=True)
        target_ref[:, lanes] = (cid[:, lanes] * CAP + place).astype(jnp.int32)
        goals.append((lower + place).astype(jnp.int32))
    rank = (code & 65535) + 1
    high = jnp.broadcast_to((rank >> 8).astype(jnp.float32), (META // 2, rows))
    low = jnp.broadcast_to((rank & 255).astype(jnp.float32), (META // 2, rows))
    both = jnp.concatenate([high, low, jnp.zeros((LANES - META, rows), jnp.float32)], axis=0)
    unit_ref[:, width:] = jnp.transpose(both).astype(jnp.bfloat16)
    chunk = 128
    for r in range(rows // chunk):
        part = slice(r * chunk, (r + 1) * chunk)
        e = emb_ref[part, :].astype(jnp.float32)
        scale = lax.rsqrt(jnp.sum(e * e, axis=1, keepdims=True) + 1e-06)
        unit_ref[part, :width] = (e * scale).astype(jnp.bfloat16)
    slot = lax.broadcasted_iota(jnp.int32, (rows, rows), 0)
    place = jnp.where(slot == jnp.concatenate(goals, axis=1), 1.0, 0.0).astype(jnp.bfloat16)
    ordered = jnp.dot(place, unit_ref[...], preferred_element_type=jnp.float32)
    for k in range(columns + 1):
        sorted_ref[k, :rows, :] = ordered[:, k * LANES : (k + 1) * LANES]
        sorted_ref[k, rows:, :] = jnp.zeros((CAP, LANES), jnp.float32)
    copy.wait()
    me = lax.axis_index("owner") % PER_ROW
    segment = lax.broadcasted_iota(jnp.int32, (META, LANES), 1) // CAP
    line = lax.broadcasted_iota(jnp.int32, (CAP, LANES), 0)
    for group in range(owners // PER_ROW):
        ranks = []
        for q in range(PER_ROW):
            c = group * PER_ROW + q
            some = pl.ds(counts_smem[0, c], CAP)
            for k in range(columns):
                out_ref[c, k * CAP : (k + 1) * CAP, :] = sorted_ref[k, some, :].astype(jnp.bfloat16)
            ranks.append(jnp.where(line < counts_smem[1, c], sorted_ref[columns, some, :], 0.0))
        tile = jnp.transpose(jnp.concatenate(ranks, axis=0))[:META, :]
        for q in range(PER_ROW):
            alone = jnp.where(segment == q, tile, 0.0)
            moved = pltpu.roll(alone, (me + PER_ROW - q) % PER_ROW * CAP, 1)
            out_ref[group * PER_ROW + q, columns * CAP :, :] = moved.astype(jnp.bfloat16)


def pack(embeddings, code, owners):
    rows, width = embeddings.shape
    return pl.pallas_call(
        pack_kernel,
        out_shape=(
            jax.ShapeDtypeStruct((owners, width // LANES * CAP + META, LANES), jnp.bfloat16),
            jax.ShapeDtypeStruct((1, rows), jnp.int32),
        ),
        in_specs=[pl.BlockSpec(memory_space=pltpu.VMEM)] * 2,
        out_specs=(pl.BlockSpec(memory_space=pltpu.VMEM),) * 2,
        scratch_shapes=[
            pltpu.VMEM((rows, width + LANES), jnp.bfloat16),
            pltpu.VMEM((width // LANES + 1, rows + CAP, LANES), jnp.float32),
            pltpu.VMEM((8, LANES), jnp.int32),
            pltpu.SMEM((8, LANES), jnp.int32),
            pltpu.SemaphoreType.DMA(()),
        ],
        compiler_params=pltpu.CompilerParams(vmem_limit_bytes=24 * 2**20),
        name="pack_rows",
    )(embeddings, code)


def rank_row(x_ref, group):
    meta = x_ref.shape[1] - META
    tiles = x_ref[group * PER_ROW : (group + 1) * PER_ROW, meta:, :].astype(jnp.float32)
    both = jnp.sum(tiles, axis=0)
    code = both[:1] * 256.0 + both[META // 2 : META // 2 + 1]
    return jnp.broadcast_to(jnp.where(code == 0.0, EMPTY, code), (8, LANES))


def as_column(row):
    return jnp.transpose(jnp.broadcast_to(row[:1], (LANES, LANES)))


def rows_of(x_ref, first, count):
    block = slice(first // CAP, (first + count) // CAP)
    columns = (x_ref.shape[1] - META) // CAP
    parts = [x_ref[block, k * CAP : (k + 1) * CAP, :].reshape(count, LANES) for k in range(columns)]
    return jnp.concatenate(parts, axis=1)


def compare(x, y, first, start, column_ref, row_ref, rows_ref, across):
    sims = lax.dot_general(x, y, (((1,), (1,)), ((), ())), preferred_element_type=jnp.float32)
    some = slice(first, first + x.shape[0])
    column = column_ref[some, :]
    best = rows_ref[some, :]
    for j in range(y.shape[0] // LANES):
        s = sims[:, j * LANES : (j + 1) * LANES]
        earlier = row_ref[:1, start + j * LANES : start + (j + 1) * LANES] < column
        best = jnp.maximum(best, jnp.where(earlier, s, -1.0))
        if across[j] is not None:
            later = jnp.where(earlier, -1.0, s)
            across[j] = jnp.maximum(across[j], jnp.max(later.reshape(-1, 8, LANES), axis=0))
    rows_ref[some, :] = best


def lowest():
    return jnp.full((8, LANES), -1.0, jnp.float32)


def own_kernel(x_ref, rows_ref, columns_ref, column_ref, row_ref):
    count = x_ref.shape[0] * CAP
    rows_ref[...] = jnp.full(rows_ref.shape, -1.0, jnp.float32)
    for g in range(count // LANES):
        lanes = slice(g * LANES, (g + 1) * LANES)
        row = rank_row(x_ref, g)
        row_ref[:, lanes] = row
        column_ref[lanes, :] = as_column(row)
    per = TILE // LANES
    for start in range(0, count, TILE):
        y = rows_of(x_ref, start, TILE)
        across = [lowest() for _ in range(per)]
        for first in range(0, start, PART):
            x = rows_of(x_ref, first, PART)
            compare(x, y, first, start, column_ref, row_ref, rows_ref, across)
        half = per // 2
        x = rows_of(x_ref, start, TILE // 2)
        some = [None] * half + across[half:]
        compare(x, y, start, start, column_ref, row_ref, rows_ref, some)
        across[half:] = some[half:]
        middle = start + TILE // 2
        x = rows_of(x_ref, middle, TILE // 2)
        compare(x, x, middle, middle, column_ref, row_ref, rows_ref, [None] * half)
        for j in range(per):
            columns_ref[:, start + j * LANES : start + (j + 1) * LANES] = across[j]


def cross(x_ref, y_ref, column_ref, row_ref, rows_ref, columns_ref):
    count = y_ref.shape[0] * CAP
    for start in range(0, count, TILE):
        y = rows_of(y_ref, start, TILE)
        lanes = [slice(start + j * LANES, start + (j + 1) * LANES) for j in range(TILE // LANES)]
        across = [columns_ref[:, part] for part in lanes]
        for first in range(0, count, PART):
            x = rows_of(x_ref, first, PART)
            compare(x, y, first, start, column_ref, row_ref, rows_ref, across)
        for part, best in zip(lanes, across):
            columns_ref[:, part] = best


def along_lanes(rows_ref, first):
    return jnp.max(jnp.transpose(rows_ref[first : first + LANES, :]), axis=0, keepdims=True)


def first_kernel(x_ref, y_ref, own_rows, own_columns, column_ref, rows_ref, columns_ref, low_ref, row_ref):
    core = lax.axis_index("split")
    blocks = y_ref.shape[0]
    half = blocks * CAP
    for g in range(half // LANES):
        row_ref[:, g * LANES : (g + 1) * LANES] = rank_row(y_ref, g)
    columns_ref[...] = jnp.full(columns_ref.shape, -1.0, jnp.float32)

    def side(first):
        rows_ref[...] = own_rows[first : first + half, :]
        x = x_ref.at[first // CAP : first // CAP + blocks]
        cross(x, y_ref, column_ref.at[first : first + half], row_ref, rows_ref, columns_ref)

    @pl.when(core == 0)
    def _():
        side(0)
        for g in range(0, half, LANES):
            low_ref[:, g : g + LANES] = jnp.broadcast_to(along_lanes(rows_ref, g), (8, LANES))
        rows_ref[...] = own_rows[half:, :]

    @pl.when(core != 0)
    def _():
        side(half)
        for g in range(0, half, LANES):
            low_ref[:, g : g + LANES] = jnp.broadcast_to(along_lanes(own_rows, g), (8, LANES))

    low_ref[...] = jnp.maximum(
        low_ref[...], jnp.max(own_columns[:, :half], axis=0, keepdims=True)
    )


def second_kernel(
    x_ref, y_ref, z_ref, low_ref, rows_in, columns_in, own_columns, column_ref, out_ref, row_ref, rows_ref, columns_ref
):
    core = lax.axis_index("split")
    blocks = y_ref.shape[0]
    half = blocks * CAP
    rows_ref[...] = rows_in[...]

    def side(other_ref):
        for g in range(half // LANES):
            row_ref[:, g * LANES : (g + 1) * LANES] = rank_row(other_ref, g)
        x = x_ref.at[blocks:]
        cross(x, other_ref, column_ref.at[half:], row_ref, rows_ref, columns_ref)

    @pl.when(core == 0)
    def _():
        columns_ref[...] = columns_in[...]
        side(y_ref)

    @pl.when(core != 0)
    def _():
        columns_ref[...] = jnp.full(columns_ref.shape, -1.0, jnp.float32)
        side(z_ref)

    parity = lax.broadcasted_iota(jnp.int32, (8, LANES), 0) % 2
    groups = half // LANES
    for g in range(2 * groups):
        a = slice(g * LANES, (g + 1) * LANES)
        b = slice(g % groups * LANES, (g % groups + 1) * LANES)
        now = jnp.max(columns_ref[:, b], axis=0, keepdims=True)
        if g < groups:
            mine = low_ref[:1, b]
            theirs = jnp.where(core == 0, now, jnp.max(columns_in[:, b], axis=0, keepdims=True))
        else:
            mine = jnp.max(own_columns[:, a], axis=0, keepdims=True)
            mine = jnp.maximum(mine, along_lanes(rows_ref, g % groups * LANES))
            theirs = jnp.where(core == 0, jnp.full((1, LANES), -1.0, jnp.float32), now)
        out_ref[g * 8 : (g + 1) * 8, :] = jnp.where(
            parity == core, jnp.broadcast_to(mine, (8, LANES)), jnp.broadcast_to(theirs, (8, LANES))
        )


def all_pairs(x, y, z, width):
    count = x.shape[0] * CAP
    half = count // 2
    cost = pl.CostEstimate(flops=2 * half * half * width, bytes_accessed=4 * half * width, transcendentals=0)
    vmem = pl.BlockSpec(memory_space=pltpu.VMEM)
    params = pltpu.CompilerParams(vmem_limit_bytes=20 * 2**20)

    def array(*dims):
        return jax.ShapeDtypeStruct(dims, jnp.float32)

    own_rows, own_columns, column = pl.pallas_call(
        own_kernel,
        out_shape=(array(count, LANES), array(8, count), array(count, LANES)),
        in_specs=[vmem],
        out_specs=(vmem,) * 3,
        scratch_shapes=[pltpu.VMEM((8, count), jnp.float32)],
        compiler_params=params,
        cost_estimate=pl.CostEstimate(
            flops=count * (count + TILE) * width, bytes_accessed=2 * count * width, transcendentals=0
        ),
        name="own_pairs",
    )(x)
    rows, columns, low = pl.pallas_call(
        first_kernel,
        out_shape=(array(half, LANES), array(8, half), array(8, half)),
        in_specs=[vmem] * 5,
        out_specs=(vmem,) * 3,
        scratch_shapes=[pltpu.VMEM((8, half), jnp.float32)],
        compiler_params=params,
        cost_estimate=cost,
        name="cross_first",
    )(x, y, own_rows, own_columns, column)
    return pl.pallas_call(
        second_kernel,
        out_shape=array(count // LANES * 8, LANES),
        in_specs=[vmem] * 8,
        out_specs=vmem,
        scratch_shapes=[
            pltpu.VMEM((8, half), jnp.float32),
            pltpu.VMEM((half, LANES), jnp.float32),
            pltpu.VMEM((8, half), jnp.float32),
        ],
        compiler_params=params,
        cost_estimate=cost,
        name="cross_second",
    )(x, y, z, low, rows, columns, own_columns, column)


def pick_kernel(recv_ref, target_ref, out_ref):
    pairs = recv_ref.shape[0]
    owners = pairs // 2
    best = jnp.maximum(
        recv_ref[pl.ds(0, owners, stride=2), :], recv_ref[pl.ds(1, owners, stride=2), :]
    )
    target = target_ref[...]
    rows = target.shape[1]
    cid = target >> 5
    slot = (target & (CAP - 1)) + lax.axis_index("owner") % PER_ROW * CAP
    chosen = lax.broadcasted_iota(jnp.int32, (owners, rows), 0) == cid
    chosen = chosen.astype(jnp.float32).astype(jnp.bfloat16)
    total = jnp.zeros((LANES, rows), jnp.float32)
    rest = best
    for _ in range(3):
        piece = rest.astype(jnp.bfloat16)
        rest = rest - piece.astype(jnp.float32)
        total += lax.dot_general(
            piece, chosen, (((0,), (0,)), ((), ())), preferred_element_type=jnp.float32
        )
    mine = lax.broadcasted_iota(jnp.int32, (LANES, rows), 0) == slot
    out_ref[...] = jnp.sum(jnp.where(mine, total, 0.0), axis=0, keepdims=True)


def pick(recv, target):
    return pl.pallas_call(
        pick_kernel,
        out_shape=jax.ShapeDtypeStruct(target.shape, jnp.float32),
        in_specs=[pl.BlockSpec(memory_space=pltpu.VMEM)] * 2,
        out_specs=pl.BlockSpec(memory_space=pltpu.VMEM),
        compiler_params=pltpu.CompilerParams(vmem_limit_bytes=8 * 2**20),
        name="pick_results",
    )(recv, target)


def shards(embeddings, cluster, order):
    owners = lax.axis_size("owner")
    rows, width = embeddings.shape
    cid, rank = lax.optimization_barrier((cluster.reshape(1, rows), order.reshape(1, rows)))
    code = cid * 65536 + rank
    packed, target = pack(embeddings, code, owners)
    mine = lax.all_to_all(packed, "owner", split_axis=0, concat_axis=0, tiled=True)
    swap = [(0, 1), (1, 0)]
    half = owners // 2
    first = lax.ppermute(mine[:half], "split", swap)
    second = lax.ppermute(mine[half:], "split", swap)
    best = all_pairs(mine, first, second, width)
    returned = lax.all_to_all(best, ("owner", "split"), split_axis=0, concat_axis=0, tiled=True)
    return pick(returned, target).reshape(rows)


def solution(mesh):
    return jax.shard_map(
        shards,
        mesh=mesh,
        in_specs=(P(("owner", "split"), None), P(("owner", "split"), None), P(("owner", "split"))),
        out_specs=P(("owner", "split")),
        check_vma=False,
    )
```

```python
import functools
import jax
import jax.numpy as jnp
from jax import lax
from jax.experimental import pallas as pl
from jax.experimental.pallas import tpu as pltpu
from jax.sharding import PartitionSpec as P

CAP = 32
LANES = 128
META = 8
EMPTY = 262144.0
TILE = 512
PART = 512
PER_TILE = TILE // CAP
PER_ROW = LANES // CAP


def pack_kernel(emb_ref, code_ref, out_ref, target_ref, unit_ref, sorted_ref, counts_ref, counts_smem, sem):
    rows, width = emb_ref.shape
    owners = out_ref.shape[0]
    columns = width // LANES
    code = code_ref[...]
    cid = (code >> 16).astype(jnp.float32)
    column = jnp.transpose(jnp.broadcast_to(cid, (LANES, rows)))
    above = lax.broadcasted_iota(jnp.int32, (LANES, LANES), 0)
    here = lax.broadcasted_iota(jnp.int32, (LANES, LANES), 1)
    before = jnp.sum(jnp.where(column < here[:1].astype(jnp.float32), 1.0, 0.0), axis=0, keepdims=True)
    number = jnp.sum(jnp.where(column == here[:1].astype(jnp.float32), 1.0, 0.0), axis=0, keepdims=True)
    counts_ref[...] = jnp.zeros(counts_ref.shape, jnp.int32)
    counts_ref[0:1, :] = before.astype(jnp.int32)
    counts_ref[1:2, :] = number.astype(jnp.int32)
    copy = pltpu.make_async_copy(counts_ref, counts_smem, sem)
    copy.start()
    goals = []
    for j in range(rows // LANES):
        lanes = slice(j * LANES, (j + 1) * LANES)
        place = jnp.zeros((1, LANES), jnp.float32)
        lower = jnp.zeros((1, LANES), jnp.float32)
        for i in range(rows // LANES):
            other = column[i * LANES : (i + 1) * LANES]
            lower += jnp.sum(jnp.where(other < cid[:, lanes], 1.0, 0.0), axis=0, keepdims=True)
            if i <= j:
                same = other == cid[:, lanes]
                if i == j:
                    same = same & (above < here)
                place += jnp.sum(jnp.where(same, 1.0, 0.0), axis=0, keepdims=True)
        target_ref[:, lanes] = (cid[:, lanes] * CAP + place).astype(jnp.int32)
        goals.append((lower + place).astype(jnp.int32))
    rank = (code & 65535) + 1
    high = jnp.broadcast_to((rank >> 8).astype(jnp.float32), (META // 2, rows))
    low = jnp.broadcast_to((rank & 255).astype(jnp.float32), (META // 2, rows))
    both = jnp.concatenate([high, low, jnp.zeros((LANES - META, rows), jnp.float32)], axis=0)
    unit_ref[:, width:] = jnp.transpose(both).astype(jnp.bfloat16)
    chunk = 128
    for r in range(rows // chunk):
        part = slice(r * chunk, (r + 1) * chunk)
        e = emb_ref[part, :].astype(jnp.float32)
        scale = lax.rsqrt(jnp.sum(e * e, axis=1, keepdims=True) + 1e-06)
        unit_ref[part, :width] = (e * scale).astype(jnp.bfloat16)
    slot = lax.broadcasted_iota(jnp.int32, (rows, rows), 0)
    place = jnp.where(slot == jnp.concatenate(goals, axis=1), 1.0, 0.0).astype(jnp.bfloat16)
    ordered = jnp.dot(place, unit_ref[...], preferred_element_type=jnp.float32)
    for k in range(columns + 1):
        sorted_ref[k, :rows, :] = ordered[:, k * LANES : (k + 1) * LANES]
        sorted_ref[k, rows:, :] = jnp.zeros((CAP, LANES), jnp.float32)
    copy.wait()
    me = lax.axis_index("owner") % PER_ROW
    segment = lax.broadcasted_iota(jnp.int32, (META, LANES), 1) // CAP
    line = lax.broadcasted_iota(jnp.int32, (CAP, LANES), 0)
    for group in range(owners // PER_ROW):
        ranks = []
        for q in range(PER_ROW):
            c = group * PER_ROW + q
            some = pl.ds(counts_smem[0, c], CAP)
            for k in range(columns):
                out_ref[c, k * CAP : (k + 1) * CAP, :] = sorted_ref[k, some, :].astype(jnp.bfloat16)
            ranks.append(jnp.where(line < counts_smem[1, c], sorted_ref[columns, some, :], 0.0))
        tile = jnp.transpose(jnp.concatenate(ranks, axis=0))[:META, :]
        for q in range(PER_ROW):
            alone = jnp.where(segment == q, tile, 0.0)
            moved = pltpu.roll(alone, (me + PER_ROW - q) % PER_ROW * CAP, 1)
            out_ref[group * PER_ROW + q, columns * CAP :, :] = moved.astype(jnp.bfloat16)


def pack(embeddings, code, owners):
    rows, width = embeddings.shape
    return pl.pallas_call(
        pack_kernel,
        out_shape=(
            jax.ShapeDtypeStruct((owners, width // LANES * CAP + META, LANES), jnp.bfloat16),
            jax.ShapeDtypeStruct((1, rows), jnp.int32),
        ),
        in_specs=[pl.BlockSpec(memory_space=pltpu.VMEM)] * 2,
        out_specs=(pl.BlockSpec(memory_space=pltpu.VMEM),) * 2,
        scratch_shapes=[
            pltpu.VMEM((rows, width + LANES), jnp.bfloat16),
            pltpu.VMEM((width // LANES + 1, rows + CAP, LANES), jnp.float32),
            pltpu.VMEM((8, LANES), jnp.int32),
            pltpu.SMEM((8, LANES), jnp.int32),
            pltpu.SemaphoreType.DMA(()),
        ],
        compiler_params=pltpu.CompilerParams(vmem_limit_bytes=24 * 2**20),
        name="pack_rows",
    )(embeddings, code)


def rank_row(x_ref, group):
    meta = x_ref.shape[1] - META
    tiles = x_ref[group * PER_ROW : (group + 1) * PER_ROW, meta:, :].astype(jnp.float32)
    both = jnp.sum(tiles, axis=0)
    code = both[:1] * 256.0 + both[META // 2 : META // 2 + 1]
    return jnp.broadcast_to(jnp.where(code == 0.0, EMPTY, code), (8, LANES))


def as_column(row):
    return jnp.transpose(jnp.broadcast_to(row[:1], (LANES, LANES)))


def rows_of(x_ref, first, count):
    block = slice(first // CAP, (first + count) // CAP)
    columns = (x_ref.shape[1] - META) // CAP
    parts = [x_ref[block, k * CAP : (k + 1) * CAP, :].reshape(count, LANES) for k in range(columns)]
    return jnp.concatenate(parts, axis=1)


def compare(x, y, first, start, column_ref, row_ref, rows_ref, across):
    sims = lax.dot_general(x, y, (((1,), (1,)), ((), ())), preferred_element_type=jnp.float32)
    some = slice(first, first + x.shape[0])
    column = column_ref[some, :]
    best = rows_ref[some, :]
    for j in range(y.shape[0] // LANES):
        s = sims[:, j * LANES : (j + 1) * LANES]
        earlier = row_ref[:1, start + j * LANES : start + (j + 1) * LANES] < column
        best = jnp.maximum(best, jnp.where(earlier, s, -1.0))
        if across[j] is not None:
            later = jnp.where(earlier, -1.0, s)
            across[j] = jnp.maximum(across[j], jnp.max(later.reshape(-1, 8, LANES), axis=0))
    rows_ref[some, :] = best


def lowest():
    return jnp.full((8, LANES), -1.0, jnp.float32)


def own_kernel(x_ref, rows_ref, columns_ref, column_ref, row_ref):
    count = x_ref.shape[0] * CAP
    rows_ref[...] = jnp.full(rows_ref.shape, -1.0, jnp.float32)
    for g in range(count // LANES):
        lanes = slice(g * LANES, (g + 1) * LANES)
        row = rank_row(x_ref, g)
        row_ref[:, lanes] = row
        column_ref[lanes, :] = as_column(row)
    per = TILE // LANES
    for start in range(0, count, TILE):
        y = rows_of(x_ref, start, TILE)
        across = [lowest() for _ in range(per)]
        for first in range(0, start, PART):
            x = rows_of(x_ref, first, PART)
            compare(x, y, first, start, column_ref, row_ref, rows_ref, across)
        half = per // 2
        x = rows_of(x_ref, start, TILE // 2)
        some = [None] * half + across[half:]
        compare(x, y, start, start, column_ref, row_ref, rows_ref, some)
        across[half:] = some[half:]
        middle = start + TILE // 2
        x = rows_of(x_ref, middle, TILE // 2)
        compare(x, x, middle, middle, column_ref, row_ref, rows_ref, [None] * half)
        for j in range(per):
            columns_ref[:, start + j * LANES : start + (j + 1) * LANES] = across[j]


def cross(x_ref, y_ref, column_ref, row_ref, rows_ref, columns_ref):
    count = y_ref.shape[0] * CAP
    for start in range(0, count, TILE):
        y = rows_of(y_ref, start, TILE)
        lanes = [slice(start + j * LANES, start + (j + 1) * LANES) for j in range(TILE // LANES)]
        across = [columns_ref[:, part] for part in lanes]
        for first in range(0, count, PART):
            x = rows_of(x_ref, first, PART)
            compare(x, y, first, start, column_ref, row_ref, rows_ref, across)
        for part, best in zip(lanes, across):
            columns_ref[:, part] = best


def along_lanes(rows_ref, first):
    return jnp.max(jnp.transpose(rows_ref[first : first + LANES, :]), axis=0, keepdims=True)


def first_kernel(x_ref, y_ref, own_rows, own_columns, column_ref, rows_ref, columns_ref, low_ref, row_ref):
    core = lax.axis_index("split")
    blocks = y_ref.shape[0]
    half = blocks * CAP
    for g in range(half // LANES):
        row_ref[:, g * LANES : (g + 1) * LANES] = rank_row(y_ref, g)
    columns_ref[...] = jnp.full(columns_ref.shape, -1.0, jnp.float32)

    def side(first):
        rows_ref[...] = own_rows[first : first + half, :]
        x = x_ref.at[first // CAP : first // CAP + blocks]
        cross(x, y_ref, column_ref.at[first : first + half], row_ref, rows_ref, columns_ref)

    @pl.when(core == 0)
    def _():
        side(0)
        for g in range(0, half, LANES):
            low_ref[:, g : g + LANES] = jnp.broadcast_to(along_lanes(rows_ref, g), (8, LANES))
        rows_ref[...] = own_rows[half:, :]

    @pl.when(core != 0)
    def _():
        side(half)
        for g in range(0, half, LANES):
            low_ref[:, g : g + LANES] = jnp.broadcast_to(along_lanes(own_rows, g), (8, LANES))

    low_ref[...] = jnp.maximum(
        low_ref[...], jnp.max(own_columns[:, :half], axis=0, keepdims=True)
    )


def second_kernel(
    x_ref, y_ref, z_ref, low_ref, rows_in, columns_in, own_columns, column_ref, out_ref, row_ref, rows_ref, columns_ref
):
    core = lax.axis_index("split")
    blocks = y_ref.shape[0]
    half = blocks * CAP
    rows_ref[...] = rows_in[...]

    def side(other_ref):
        for g in range(half // LANES):
            row_ref[:, g * LANES : (g + 1) * LANES] = rank_row(other_ref, g)
        x = x_ref.at[blocks:]
        cross(x, other_ref, column_ref.at[half:], row_ref, rows_ref, columns_ref)

    @pl.when(core == 0)
    def _():
        columns_ref[...] = columns_in[...]
        side(y_ref)

    @pl.when(core != 0)
    def _():
        columns_ref[...] = jnp.full(columns_ref.shape, -1.0, jnp.float32)
        side(z_ref)

    parity = lax.broadcasted_iota(jnp.int32, (8, LANES), 0) % 2
    groups = half // LANES
    for g in range(2 * groups):
        a = slice(g * LANES, (g + 1) * LANES)
        b = slice(g % groups * LANES, (g % groups + 1) * LANES)
        now = jnp.max(columns_ref[:, b], axis=0, keepdims=True)
        if g < groups:
            mine = low_ref[:1, b]
            theirs = jnp.where(core == 0, now, jnp.max(columns_in[:, b], axis=0, keepdims=True))
        else:
            mine = jnp.max(own_columns[:, a], axis=0, keepdims=True)
            mine = jnp.maximum(mine, along_lanes(rows_ref, g % groups * LANES))
            theirs = jnp.where(core == 0, jnp.full((1, LANES), -1.0, jnp.float32), now)
        out_ref[g * 8 : (g + 1) * 8, :] = jnp.where(
            parity == core, jnp.broadcast_to(mine, (8, LANES)), jnp.broadcast_to(theirs, (8, LANES))
        )


def all_pairs(x, y, z, width):
    count = x.shape[0] * CAP
    half = count // 2
    cost = pl.CostEstimate(flops=2 * half * half * width, bytes_accessed=4 * half * width, transcendentals=0)
    vmem = pl.BlockSpec(memory_space=pltpu.VMEM)
    params = pltpu.CompilerParams(vmem_limit_bytes=20 * 2**20)

    def array(*dims):
        return jax.ShapeDtypeStruct(dims, jnp.float32)

    own_rows, own_columns, column = pl.pallas_call(
        own_kernel,
        out_shape=(array(count, LANES), array(8, count), array(count, LANES)),
        in_specs=[vmem],
        out_specs=(vmem,) * 3,
        scratch_shapes=[pltpu.VMEM((8, count), jnp.float32)],
        compiler_params=params,
        cost_estimate=pl.CostEstimate(
            flops=count * (count + TILE) * width, bytes_accessed=2 * count * width, transcendentals=0
        ),
        name="own_pairs",
    )(x)
    rows, columns, low = pl.pallas_call(
        first_kernel,
        out_shape=(array(half, LANES), array(8, half), array(8, half)),
        in_specs=[vmem] * 5,
        out_specs=(vmem,) * 3,
        scratch_shapes=[pltpu.VMEM((8, half), jnp.float32)],
        compiler_params=params,
        cost_estimate=cost,
        name="cross_first",
    )(x, y, own_rows, own_columns, column)
    return pl.pallas_call(
        second_kernel,
        out_shape=array(count // LANES * 8, LANES),
        in_specs=[vmem] * 8,
        out_specs=vmem,
        scratch_shapes=[
            pltpu.VMEM((8, half), jnp.float32),
            pltpu.VMEM((half, LANES), jnp.float32),
            pltpu.VMEM((8, half), jnp.float32),
        ],
        compiler_params=params,
        cost_estimate=cost,
        name="cross_second",
    )(x, y, z, low, rows, columns, own_columns, column)


def pick_kernel(recv_ref, target_ref, out_ref):
    pairs = recv_ref.shape[0]
    owners = pairs // 2
    best = jnp.maximum(
        recv_ref[pl.ds(0, owners, stride=2), :], recv_ref[pl.ds(1, owners, stride=2), :]
    )
    target = target_ref[...]
    rows = target.shape[1]
    cid = target >> 5
    slot = (target & (CAP - 1)) + lax.axis_index("owner") % PER_ROW * CAP
    chosen = lax.broadcasted_iota(jnp.int32, (owners, rows), 0) == cid
    chosen = jnp.where(chosen, 1.0, 0.0).astype(jnp.bfloat16)
    pieces, rest = [], best
    for _ in range(3):
        pieces.append(rest.astype(jnp.bfloat16))
        rest = rest - pieces[-1].astype(jnp.float32)
    total = lax.dot_general(
        jnp.concatenate(pieces, axis=0), jnp.concatenate([chosen] * 3, axis=0),
        (((0,), (0,)), ((), ())), preferred_element_type=jnp.float32,
    )
    mine = lax.broadcasted_iota(jnp.int32, (LANES, rows), 0) == slot
    out_ref[...] = jnp.sum(jnp.where(mine, total, 0.0), axis=0, keepdims=True)


def pick(recv, target):
    return pl.pallas_call(
        pick_kernel,
        out_shape=jax.ShapeDtypeStruct(target.shape, jnp.float32),
        in_specs=[pl.BlockSpec(memory_space=pltpu.VMEM)] * 2,
        out_specs=pl.BlockSpec(memory_space=pltpu.VMEM),
        compiler_params=pltpu.CompilerParams(vmem_limit_bytes=8 * 2**20),
        name="pick_results",
    )(recv, target)


def shards(embeddings, cluster, order):
    owners = lax.axis_size("owner")
    rows, width = embeddings.shape
    cid, rank = lax.optimization_barrier((cluster.reshape(1, rows), order.reshape(1, rows)))
    code = cid * 65536 + rank
    packed, target = pack(embeddings, code, owners)
    mine = lax.all_to_all(packed, "owner", split_axis=0, concat_axis=0, tiled=True)
    swap = [(0, 1), (1, 0)]
    half = owners // 2
    first = lax.ppermute(mine[:half], "split", swap)
    second = lax.ppermute(mine[half:], "split", swap)
    best = all_pairs(mine, first, second, width)
    returned = lax.all_to_all(best, ("owner", "split"), split_axis=0, concat_axis=0, tiled=True)
    return pick(returned, target).reshape(rows)


def solution(mesh):
    return jax.shard_map(
        shards,
        mesh=mesh,
        in_specs=(P(("owner", "split"), None), P(("owner", "split"), None), P(("owner", "split"))),
        out_specs=P(("owner", "split")),
        check_vma=False,
    )
```

```python
import functools
import jax
import jax.numpy as jnp
from jax import lax
from jax.experimental import pallas as pl
from jax.experimental.pallas import tpu as pltpu
from jax.sharding import PartitionSpec as P

CAP = 32
LANES = 128
META = 8
EMPTY = 262144.0
TILE = 512
PART = 512
PER_TILE = TILE // CAP
PER_ROW = LANES // CAP


def pack_kernel(emb_ref, code_ref, out_ref, target_ref, unit_ref, sorted_ref, counts_ref, counts_smem, sem):
    rows, width = emb_ref.shape
    owners = out_ref.shape[0]
    columns = width // LANES
    code = code_ref[...]
    cid = (code >> 16).astype(jnp.float32)
    column = jnp.transpose(jnp.broadcast_to(cid, (LANES, rows)))
    above = lax.broadcasted_iota(jnp.int32, (LANES, LANES), 0)
    here = lax.broadcasted_iota(jnp.int32, (LANES, LANES), 1)
    before = jnp.sum(jnp.where(column < here[:1].astype(jnp.float32), 1.0, 0.0), axis=0, keepdims=True)
    number = jnp.sum(jnp.where(column == here[:1].astype(jnp.float32), 1.0, 0.0), axis=0, keepdims=True)
    counts_ref[...] = jnp.zeros(counts_ref.shape, jnp.int32)
    counts_ref[0:1, :] = before.astype(jnp.int32)
    counts_ref[1:2, :] = number.astype(jnp.int32)
    copy = pltpu.make_async_copy(counts_ref, counts_smem, sem)
    copy.start()
    goals = []
    for j in range(rows // LANES):
        lanes = slice(j * LANES, (j + 1) * LANES)
        place = jnp.zeros((1, LANES), jnp.float32)
        lower = jnp.zeros((1, LANES), jnp.float32)
        for i in range(rows // LANES):
            other = column[i * LANES : (i + 1) * LANES]
            lower += jnp.sum(jnp.where(other < cid[:, lanes], 1.0, 0.0), axis=0, keepdims=True)
            if i <= j:
                same = other == cid[:, lanes]
                if i == j:
                    same = same & (above < here)
                place += jnp.sum(jnp.where(same, 1.0, 0.0), axis=0, keepdims=True)
        target_ref[:, lanes] = (cid[:, lanes] * CAP + place).astype(jnp.int32)
        goals.append((lower + place).astype(jnp.int32))
    rank = ((code & 65535) + 1).astype(jnp.float32)
    goal = jnp.concatenate(goals, axis=1)
    goal_column = jnp.transpose(jnp.broadcast_to(goal.astype(jnp.float32), (LANES, rows)))
    rank_column = jnp.transpose(jnp.broadcast_to(rank, (LANES, rows)))
    held = []
    for j in range(rows // LANES):
        spot = (here[:1] + j * LANES).astype(jnp.float32)
        held.append(jnp.sum(jnp.where(goal_column == spot, rank_column, 0.0), axis=0, keepdims=True))
    held = jnp.concatenate(held, axis=1).astype(jnp.int32)
    high = jnp.broadcast_to((held >> 8).astype(jnp.float32), (META // 2, rows))
    low = jnp.broadcast_to((held & 255).astype(jnp.float32), (META // 2, rows))
    ranks = jnp.concatenate([high, low], axis=0)
    chunk = 128
    for r in range(rows // chunk):
        part = slice(r * chunk, (r + 1) * chunk)
        e = emb_ref[part, :].astype(jnp.float32)
        scale = lax.rsqrt(jnp.sum(e * e, axis=1, keepdims=True) + 1e-06)
        unit_ref[part, :] = (e * scale).astype(jnp.bfloat16)
    slot = lax.broadcasted_iota(jnp.int32, (rows, rows), 0)
    place = jnp.where(slot == goal, 1.0, 0.0).astype(jnp.bfloat16)
    ordered = jnp.dot(place, unit_ref[...], preferred_element_type=jnp.float32)
    for k in range(columns):
        sorted_ref[k, :rows, :] = ordered[:, k * LANES : (k + 1) * LANES]
        sorted_ref[k, rows:, :] = jnp.zeros((CAP, LANES), jnp.float32)
    copy.wait()
    first = lax.axis_index("owner") % PER_ROW * CAP
    lane = lax.broadcasted_iota(jnp.int32, (META, LANES), 1) - first
    for c in range(owners):
        start, count = counts_smem[0, c], counts_smem[1, c]
        for k in range(columns):
            out_ref[c, k * CAP : (k + 1) * CAP, :] = sorted_ref[k, pl.ds(start, CAP), :].astype(jnp.bfloat16)
        moved = pltpu.roll(ranks, (first + rows - start) & (rows - 1), 1)[:, :LANES]
        tile = jnp.where((lane >= 0) & (lane < count), moved, 0.0)
        out_ref[c, columns * CAP :, :] = tile.astype(jnp.bfloat16)


def pack(embeddings, code, owners):
    rows, width = embeddings.shape
    return pl.pallas_call(
        pack_kernel,
        out_shape=(
            jax.ShapeDtypeStruct((owners, width // LANES * CAP + META, LANES), jnp.bfloat16),
            jax.ShapeDtypeStruct((1, rows), jnp.int32),
        ),
        in_specs=[pl.BlockSpec(memory_space=pltpu.VMEM)] * 2,
        out_specs=(pl.BlockSpec(memory_space=pltpu.VMEM),) * 2,
        scratch_shapes=[
            pltpu.VMEM((rows, width), jnp.bfloat16),
            pltpu.VMEM((width // LANES, rows + CAP, LANES), jnp.float32),
            pltpu.VMEM((8, LANES), jnp.int32),
            pltpu.SMEM((8, LANES), jnp.int32),
            pltpu.SemaphoreType.DMA(()),
        ],
        compiler_params=pltpu.CompilerParams(vmem_limit_bytes=24 * 2**20),
        name="pack_rows",
    )(embeddings, code)


def rank_row(x_ref, group):
    meta = x_ref.shape[1] - META
    tiles = x_ref[group * PER_ROW : (group + 1) * PER_ROW, meta:, :].astype(jnp.float32)
    both = jnp.sum(tiles, axis=0)
    code = both[:1] * 256.0 + both[META // 2 : META // 2 + 1]
    return jnp.broadcast_to(jnp.where(code == 0.0, EMPTY, code), (8, LANES))


def as_column(row):
    return jnp.transpose(jnp.broadcast_to(row[:1], (LANES, LANES)))


def rows_of(x_ref, first, count):
    block = slice(first // CAP, (first + count) // CAP)
    columns = (x_ref.shape[1] - META) // CAP
    parts = [x_ref[block, k * CAP : (k + 1) * CAP, :].reshape(count, LANES) for k in range(columns)]
    return jnp.concatenate(parts, axis=1)


def compare(x, y, first, start, column_ref, row_ref, rows_ref, across):
    sims = lax.dot_general(x, y, (((1,), (1,)), ((), ())), preferred_element_type=jnp.float32)
    some = slice(first, first + x.shape[0])
    column = column_ref[some, :]
    best = rows_ref[some, :]
    for j in range(y.shape[0] // LANES):
        s = sims[:, j * LANES : (j + 1) * LANES]
        earlier = row_ref[:1, start + j * LANES : start + (j + 1) * LANES] < column
        best = jnp.maximum(best, jnp.where(earlier, s, -1.0))
        if across[j] is not None:
            later = jnp.where(earlier, -1.0, s)
            across[j] = jnp.maximum(across[j], jnp.max(later.reshape(-1, 8, LANES), axis=0))
    rows_ref[some, :] = best


def lowest():
    return jnp.full((8, LANES), -1.0, jnp.float32)


def own_kernel(x_ref, rows_ref, columns_ref, column_ref, row_ref):
    count = x_ref.shape[0] * CAP
    rows_ref[...] = jnp.full(rows_ref.shape, -1.0, jnp.float32)
    for g in range(count // LANES):
        lanes = slice(g * LANES, (g + 1) * LANES)
        row = rank_row(x_ref, g)
        row_ref[:, lanes] = row
        column_ref[lanes, :] = as_column(row)
    per = TILE // LANES
    for start in range(0, count, TILE):
        y = rows_of(x_ref, start, TILE)
        across = [lowest() for _ in range(per)]
        for first in range(0, start, PART):
            x = rows_of(x_ref, first, PART)
            compare(x, y, first, start, column_ref, row_ref, rows_ref, across)
        half = per // 2
        x = rows_of(x_ref, start, TILE // 2)
        some = [None] * half + across[half:]
        compare(x, y, start, start, column_ref, row_ref, rows_ref, some)
        across[half:] = some[half:]
        middle = start + TILE // 2
        x = rows_of(x_ref, middle, TILE // 2)
        compare(x, x, middle, middle, column_ref, row_ref, rows_ref, [None] * half)
        for j in range(per):
            columns_ref[:, start + j * LANES : start + (j + 1) * LANES] = across[j]


def cross(x_ref, y_ref, column_ref, row_ref, rows_ref, columns_ref):
    count = y_ref.shape[0] * CAP
    for start in range(0, count, TILE):
        y = rows_of(y_ref, start, TILE)
        lanes = [slice(start + j * LANES, start + (j + 1) * LANES) for j in range(TILE // LANES)]
        across = [columns_ref[:, part] for part in lanes]
        for first in range(0, count, PART):
            x = rows_of(x_ref, first, PART)
            compare(x, y, first, start, column_ref, row_ref, rows_ref, across)
        for part, best in zip(lanes, across):
            columns_ref[:, part] = best


def along_lanes(rows_ref, first):
    return jnp.max(jnp.transpose(rows_ref[first : first + LANES, :]), axis=0, keepdims=True)


def first_kernel(x_ref, y_ref, own_rows, own_columns, column_ref, rows_ref, columns_ref, low_ref, row_ref):
    core = lax.axis_index("split")
    blocks = y_ref.shape[0]
    half = blocks * CAP
    for g in range(half // LANES):
        row_ref[:, g * LANES : (g + 1) * LANES] = rank_row(y_ref, g)
    columns_ref[...] = jnp.full(columns_ref.shape, -1.0, jnp.float32)

    def side(first):
        rows_ref[...] = own_rows[first : first + half, :]
        x = x_ref.at[first // CAP : first // CAP + blocks]
        cross(x, y_ref, column_ref.at[first : first + half], row_ref, rows_ref, columns_ref)

    @pl.when(core == 0)
    def _():
        side(0)
        for g in range(0, half, LANES):
            low_ref[:, g : g + LANES] = jnp.broadcast_to(along_lanes(rows_ref, g), (8, LANES))
        rows_ref[...] = own_rows[half:, :]

    @pl.when(core != 0)
    def _():
        side(half)
        for g in range(0, half, LANES):
            low_ref[:, g : g + LANES] = jnp.broadcast_to(along_lanes(own_rows, g), (8, LANES))

    low_ref[...] = jnp.maximum(
        low_ref[...], jnp.max(own_columns[:, :half], axis=0, keepdims=True)
    )


def second_kernel(
    x_ref, y_ref, z_ref, low_ref, rows_in, columns_in, own_columns, column_ref, out_ref, row_ref, rows_ref, columns_ref
):
    core = lax.axis_index("split")
    blocks = y_ref.shape[0]
    half = blocks * CAP
    rows_ref[...] = rows_in[...]

    def side(other_ref):
        for g in range(half // LANES):
            row_ref[:, g * LANES : (g + 1) * LANES] = rank_row(other_ref, g)
        x = x_ref.at[blocks:]
        cross(x, other_ref, column_ref.at[half:], row_ref, rows_ref, columns_ref)

    @pl.when(core == 0)
    def _():
        columns_ref[...] = columns_in[...]
        side(y_ref)

    @pl.when(core != 0)
    def _():
        columns_ref[...] = jnp.full(columns_ref.shape, -1.0, jnp.float32)
        side(z_ref)

    parity = lax.broadcasted_iota(jnp.int32, (8, LANES), 0) % 2
    groups = half // LANES
    for g in range(2 * groups):
        a = slice(g * LANES, (g + 1) * LANES)
        b = slice(g % groups * LANES, (g % groups + 1) * LANES)
        now = jnp.max(columns_ref[:, b], axis=0, keepdims=True)
        if g < groups:
            mine = low_ref[:1, b]
            theirs = jnp.where(core == 0, now, jnp.max(columns_in[:, b], axis=0, keepdims=True))
        else:
            mine = jnp.max(own_columns[:, a], axis=0, keepdims=True)
            mine = jnp.maximum(mine, along_lanes(rows_ref, g % groups * LANES))
            theirs = jnp.where(core == 0, jnp.full((1, LANES), -1.0, jnp.float32), now)
        out_ref[g * 8 : (g + 1) * 8, :] = jnp.where(
            parity == core, jnp.broadcast_to(mine, (8, LANES)), jnp.broadcast_to(theirs, (8, LANES))
        )


def all_pairs(x, y, z, width):
    count = x.shape[0] * CAP
    half = count // 2
    cost = pl.CostEstimate(flops=2 * half * half * width, bytes_accessed=4 * half * width, transcendentals=0)
    vmem = pl.BlockSpec(memory_space=pltpu.VMEM)
    params = pltpu.CompilerParams(vmem_limit_bytes=20 * 2**20)

    def array(*dims):
        return jax.ShapeDtypeStruct(dims, jnp.float32)

    own_rows, own_columns, column = pl.pallas_call(
        own_kernel,
        out_shape=(array(count, LANES), array(8, count), array(count, LANES)),
        in_specs=[vmem],
        out_specs=(vmem,) * 3,
        scratch_shapes=[pltpu.VMEM((8, count), jnp.float32)],
        compiler_params=params,
        cost_estimate=pl.CostEstimate(
            flops=count * (count + TILE) * width, bytes_accessed=2 * count * width, transcendentals=0
        ),
        name="own_pairs",
    )(x)
    rows, columns, low = pl.pallas_call(
        first_kernel,
        out_shape=(array(half, LANES), array(8, half), array(8, half)),
        in_specs=[vmem] * 5,
        out_specs=(vmem,) * 3,
        scratch_shapes=[pltpu.VMEM((8, half), jnp.float32)],
        compiler_params=params,
        cost_estimate=cost,
        name="cross_first",
    )(x, y, own_rows, own_columns, column)
    return pl.pallas_call(
        second_kernel,
        out_shape=array(count // LANES * 8, LANES),
        in_specs=[vmem] * 8,
        out_specs=vmem,
        scratch_shapes=[
            pltpu.VMEM((8, half), jnp.float32),
            pltpu.VMEM((half, LANES), jnp.float32),
            pltpu.VMEM((8, half), jnp.float32),
        ],
        compiler_params=params,
        cost_estimate=cost,
        name="cross_second",
    )(x, y, z, low, rows, columns, own_columns, column)


def pick_kernel(recv_ref, target_ref, out_ref):
    pairs = recv_ref.shape[0]
    owners = pairs // 2
    best = jnp.maximum(
        recv_ref[pl.ds(0, owners, stride=2), :], recv_ref[pl.ds(1, owners, stride=2), :]
    )
    target = target_ref[...]
    rows = target.shape[1]
    cid = target >> 5
    slot = (target & (CAP - 1)) + lax.axis_index("owner") % PER_ROW * CAP
    chosen = lax.broadcasted_iota(jnp.int32, (owners, rows), 0) == cid
    chosen = chosen.astype(jnp.float32).astype(jnp.bfloat16)
    total = jnp.zeros((LANES, rows), jnp.float32)
    rest = best
    for _ in range(3):
        piece = rest.astype(jnp.bfloat16)
        rest = rest - piece.astype(jnp.float32)
        total += lax.dot_general(
            piece, chosen, (((0,), (0,)), ((), ())), preferred_element_type=jnp.float32
        )
    mine = lax.broadcasted_iota(jnp.int32, (LANES, rows), 0) == slot
    out_ref[...] = jnp.sum(jnp.where(mine, total, 0.0), axis=0, keepdims=True)


def pick(recv, target):
    return pl.pallas_call(
        pick_kernel,
        out_shape=jax.ShapeDtypeStruct(target.shape, jnp.float32),
        in_specs=[pl.BlockSpec(memory_space=pltpu.VMEM)] * 2,
        out_specs=pl.BlockSpec(memory_space=pltpu.VMEM),
        compiler_params=pltpu.CompilerParams(vmem_limit_bytes=8 * 2**20),
        name="pick_results",
    )(recv, target)


def shards(embeddings, cluster, order):
    owners = lax.axis_size("owner")
    rows, width = embeddings.shape
    cid, rank = lax.optimization_barrier((cluster.reshape(1, rows), order.reshape(1, rows)))
    code = cid * 65536 + rank
    packed, target = pack(embeddings, code, owners)
    mine = lax.all_to_all(packed, "owner", split_axis=0, concat_axis=0, tiled=True)
    swap = [(0, 1), (1, 0)]
    half = owners // 2
    first = lax.ppermute(mine[:half], "split", swap)
    second = lax.ppermute(mine[half:], "split", swap)
    best = all_pairs(mine, first, second, width)
    returned = lax.all_to_all(best, ("owner", "split"), split_axis=0, concat_axis=0, tiled=True)
    return pick(returned, target).reshape(rows)


def solution(mesh):
    return jax.shard_map(
        shards,
        mesh=mesh,
        in_specs=(P(("owner", "split"), None), P(("owner", "split"), None), P(("owner", "split"))),
        out_specs=P(("owner", "split")),
        check_vma=False,
    )
```

```python
import functools
import jax
import jax.numpy as jnp
from jax import lax
from jax.experimental import pallas as pl
from jax.experimental.pallas import tpu as pltpu
from jax.sharding import PartitionSpec as P

CAP = 32
LANES = 128
META = 8
EMPTY = 262144.0
TILE = 512
PART = 512
PER_TILE = TILE // CAP
PER_ROW = LANES // CAP


def pack_kernel(emb_ref, code_ref, out_ref, target_ref, unit_ref, sorted_ref, counts_ref, counts_smem, sem):
    rows, width = emb_ref.shape
    owners = out_ref.shape[0]
    columns = width // LANES
    code = code_ref[...]
    cid = (code >> 16).astype(jnp.float32)
    column = jnp.transpose(jnp.broadcast_to(cid, (LANES, rows)))
    above = lax.broadcasted_iota(jnp.int32, (LANES, LANES), 0)
    here = lax.broadcasted_iota(jnp.int32, (LANES, LANES), 1)
    before = jnp.sum(jnp.where(column < here[:1].astype(jnp.float32), 1.0, 0.0), axis=0, keepdims=True)
    number = jnp.sum(jnp.where(column == here[:1].astype(jnp.float32), 1.0, 0.0), axis=0, keepdims=True)
    counts_ref[...] = jnp.zeros(counts_ref.shape, jnp.int32)
    counts_ref[0:1, :] = before.astype(jnp.int32)
    counts_ref[1:2, :] = number.astype(jnp.int32)
    copy = pltpu.make_async_copy(counts_ref, counts_smem, sem)
    copy.start()
    goals = []
    for j in range(rows // LANES):
        lanes = slice(j * LANES, (j + 1) * LANES)
        place = jnp.zeros((1, LANES), jnp.float32)
        lower = jnp.zeros((1, LANES), jnp.float32)
        for i in range(rows // LANES):
            other = column[i * LANES : (i + 1) * LANES]
            lower += jnp.sum(jnp.where(other < cid[:, lanes], 1.0, 0.0), axis=0, keepdims=True)
            if i <= j:
                same = other == cid[:, lanes]
                if i == j:
                    same = same & (above < here)
                place += jnp.sum(jnp.where(same, 1.0, 0.0), axis=0, keepdims=True)
        target_ref[:, lanes] = (cid[:, lanes] * CAP + place).astype(jnp.int32)
        goals.append((lower + place).astype(jnp.int32))
    rank = ((code & 65535) + 1).astype(jnp.float32)
    goal = jnp.concatenate(goals, axis=1)
    goal_column = jnp.transpose(jnp.broadcast_to(goal.astype(jnp.float32), (LANES, rows)))
    rank_column = jnp.transpose(jnp.broadcast_to(rank, (LANES, rows)))
    held = []
    for j in range(rows // LANES):
        spot = (here[:1] + j * LANES).astype(jnp.float32)
        held.append(jnp.sum(jnp.where(goal_column == spot, rank_column, 0.0), axis=0, keepdims=True))
    held = jnp.concatenate(held, axis=1).astype(jnp.int32)
    high = jnp.broadcast_to((held >> 8).astype(jnp.float32), (META // 2, rows))
    low = jnp.broadcast_to((held & 255).astype(jnp.float32), (META // 2, rows))
    ranks = jnp.concatenate([high, low], axis=0)
    chunk = 128
    for r in range(rows // chunk):
        part = slice(r * chunk, (r + 1) * chunk)
        e = emb_ref[part, :].astype(jnp.float32)
        scale = lax.rsqrt(jnp.sum(e * e, axis=1, keepdims=True) + 1e-06)
        unit_ref[part, :] = (e * scale).astype(jnp.bfloat16)
    slot = lax.broadcasted_iota(jnp.int32, (rows, rows), 0)
    place = jnp.where(slot == goal, 1.0, 0.0).astype(jnp.bfloat16)
    ordered = jnp.dot(place, unit_ref[...], preferred_element_type=jnp.float32)
    for k in range(columns):
        sorted_ref[k, :rows, :] = ordered[:, k * LANES : (k + 1) * LANES]
        sorted_ref[k, rows:, :] = jnp.zeros((CAP, LANES), jnp.float32)
    copy.wait()
    first = lax.axis_index("owner") % PER_ROW * CAP
    lane = lax.broadcasted_iota(jnp.int32, (META, LANES), 1) - first
    for c in range(owners):
        start, count = counts_smem[0, c], counts_smem[1, c]
        for k in range(columns):
            out_ref[c, k * CAP : (k + 1) * CAP, :] = sorted_ref[k, pl.ds(start, CAP), :].astype(jnp.bfloat16)
        moved = pltpu.roll(ranks, (first + rows - start) & (rows - 1), 1)[:, :LANES]
        tile = jnp.where((lane >= 0) & (lane < count), moved, 0.0)
        out_ref[c, columns * CAP :, :] = tile.astype(jnp.bfloat16)


def pack(embeddings, code, owners):
    rows, width = embeddings.shape
    return pl.pallas_call(
        pack_kernel,
        out_shape=(
            jax.ShapeDtypeStruct((owners, width // LANES * CAP + META, LANES), jnp.bfloat16),
            jax.ShapeDtypeStruct((1, rows), jnp.int32),
        ),
        in_specs=[pl.BlockSpec(memory_space=pltpu.VMEM)] * 2,
        out_specs=(pl.BlockSpec(memory_space=pltpu.VMEM),) * 2,
        scratch_shapes=[
            pltpu.VMEM((rows, width), jnp.bfloat16),
            pltpu.VMEM((width // LANES, rows + CAP, LANES), jnp.float32),
            pltpu.VMEM((8, LANES), jnp.int32),
            pltpu.SMEM((8, LANES), jnp.int32),
            pltpu.SemaphoreType.DMA(()),
        ],
        compiler_params=pltpu.CompilerParams(vmem_limit_bytes=24 * 2**20),
        name="pack_rows",
    )(embeddings, code)


def rank_row(x_ref, group):
    meta = x_ref.shape[1] - META
    tiles = x_ref[group * PER_ROW : (group + 1) * PER_ROW, meta:, :].astype(jnp.float32)
    both = jnp.sum(tiles, axis=0)
    code = both[:1] * 256.0 + both[META // 2 : META // 2 + 1]
    return jnp.broadcast_to(jnp.where(code == 0.0, EMPTY, code), (8, LANES))


def as_column(row):
    return jnp.transpose(jnp.broadcast_to(row[:1], (LANES, LANES)))


def rows_of(x_ref, first, count):
    block = slice(first // CAP, (first + count) // CAP)
    columns = (x_ref.shape[1] - META) // CAP
    parts = [x_ref[block, k * CAP : (k + 1) * CAP, :].reshape(count, LANES) for k in range(columns)]
    return jnp.concatenate(parts, axis=1)


def compare(x, y, first, start, column_ref, row_ref, rows_ref, across):
    sims = lax.dot_general(x, y, (((1,), (1,)), ((), ())), preferred_element_type=jnp.float32)
    some = slice(first, first + x.shape[0])
    column = column_ref[some, :]
    best = rows_ref[some, :]
    for j in range(y.shape[0] // LANES):
        s = sims[:, j * LANES : (j + 1) * LANES]
        earlier = row_ref[:1, start + j * LANES : start + (j + 1) * LANES] < column
        best = jnp.maximum(best, jnp.where(earlier, s, -1.0))
        if across[j] is not None:
            later = jnp.where(earlier, -1.0, s)
            across[j] = jnp.maximum(across[j], jnp.max(later.reshape(-1, 8, LANES), axis=0))
    rows_ref[some, :] = best


def lowest():
    return jnp.full((8, LANES), -1.0, jnp.float32)


def own_kernel(x_ref, out_ref, column_ref, row_ref, rows_ref, columns_ref):
    count = x_ref.shape[0] * CAP
    rows_ref[...] = jnp.full(rows_ref.shape, -1.0, jnp.float32)
    for g in range(count // LANES):
        lanes = slice(g * LANES, (g + 1) * LANES)
        row = rank_row(x_ref, g)
        row_ref[:, lanes] = row
        column_ref[lanes, :] = as_column(row)
    per = TILE // LANES
    for start in range(0, count, TILE):
        y = rows_of(x_ref, start, TILE)
        across = [lowest() for _ in range(per)]
        for first in range(0, start, PART):
            x = rows_of(x_ref, first, PART)
            compare(x, y, first, start, column_ref, row_ref, rows_ref, across)
        half = per // 2
        x = rows_of(x_ref, start, TILE // 2)
        some = [None] * half + across[half:]
        compare(x, y, start, start, column_ref, row_ref, rows_ref, some)
        across[half:] = some[half:]
        middle = start + TILE // 2
        x = rows_of(x_ref, middle, TILE // 2)
        compare(x, x, middle, middle, column_ref, row_ref, rows_ref, [None] * half)
        for j in range(per):
            columns_ref[:, start + j * LANES : start + (j + 1) * LANES] = across[j]
    for g in range(count // LANES):
        a = slice(g * LANES, (g + 1) * LANES)
        best = jnp.max(jnp.transpose(rows_ref[a, :]), axis=0, keepdims=True)
        best = jnp.maximum(best, jnp.max(columns_ref[:, a], axis=0, keepdims=True))
        out_ref[:, a] = jnp.broadcast_to(best, (8, LANES))


def own_pairs(x, width):
    owners = x.shape[0]
    count = owners * CAP
    return pl.pallas_call(
        own_kernel,
        out_shape=jax.ShapeDtypeStruct((8, count), jnp.float32),
        in_specs=[pl.BlockSpec(memory_space=pltpu.VMEM)],
        out_specs=pl.BlockSpec(memory_space=pltpu.VMEM),
        scratch_shapes=[
            pltpu.VMEM((count, LANES), jnp.float32),
            pltpu.VMEM((8, count), jnp.float32),
            pltpu.VMEM((count, LANES), jnp.float32),
            pltpu.VMEM((8, count), jnp.float32),
        ],
        compiler_params=pltpu.CompilerParams(vmem_limit_bytes=24 * 2**20),
        cost_estimate=pl.CostEstimate(
            flops=count * (count + TILE) * width, bytes_accessed=2 * count * width, transcendentals=0
        ),
        name="own_pairs",
    )(x)


def cross(all_ref, some_ref, column_ref, row_ref, rows_ref, columns_ref):
    count = all_ref.shape[0] * CAP
    rows_ref[...] = jnp.full(rows_ref.shape, -1.0, jnp.float32)
    for g in range(count // LANES):
        lanes = slice(g * LANES, (g + 1) * LANES)
        column_ref[lanes, :] = as_column(rank_row(all_ref, g))
        row_ref[:, lanes] = rank_row(some_ref, g)
    for start in range(0, count, TILE):
        y = rows_of(some_ref, start, TILE)
        lanes = [slice(start + j * LANES, start + (j + 1) * LANES) for j in range(TILE // LANES)]
        across = [columns_ref[:, part] for part in lanes]
        for first in range(0, count, PART):
            x = rows_of(all_ref, first, PART)
            compare(x, y, first, start, column_ref, row_ref, rows_ref, across)
        for part, best in zip(lanes, across):
            columns_ref[:, part] = best


def first_kernel(x_ref, y_ref, rows_out, columns_out, column_ref, row_ref, rows_ref):
    core = lax.axis_index("split")
    half = y_ref.shape[0]
    columns_out[...] = jnp.full(columns_out.shape, -1.0, jnp.float32)

    @pl.when(core == 0)
    def _():
        cross(x_ref.at[:half], y_ref, column_ref, row_ref, rows_ref, columns_out)

    @pl.when(core != 0)
    def _():
        cross(y_ref, x_ref.at[half:], column_ref, row_ref, rows_ref, columns_out)

    for g in range(half * CAP // LANES):
        a = slice(g * LANES, (g + 1) * LANES)
        best = jnp.max(jnp.transpose(rows_ref[a, :]), axis=0, keepdims=True)
        rows_out[:, a] = jnp.broadcast_to(best, (8, LANES))


def second_kernel(
    x_ref, y_ref, z_ref, own_ref, first_ref, columns_in, out_ref, column_ref, row_ref, rows_ref, columns_ref
):
    core = lax.axis_index("split")
    half = y_ref.shape[0]
    columns_ref[...] = columns_in[...]

    @pl.when(core == 0)
    def _():
        cross(x_ref.at[half:], y_ref, column_ref, row_ref, rows_ref, columns_ref)

    @pl.when(core != 0)
    def _():
        cross(z_ref, x_ref.at[half:], column_ref, row_ref, rows_ref, columns_ref)

    parity = lax.broadcasted_iota(jnp.int32, (8, LANES), 0) % 2
    groups = half * CAP // LANES
    nothing = jnp.full((1, LANES), -1.0, jnp.float32)
    for g in range(2 * groups):
        a = slice(g * LANES, (g + 1) * LANES)
        b = slice(g % groups * LANES, (g % groups + 1) * LANES)
        if g < groups:
            from_all = first_ref[:1, b]
        else:
            from_all = jnp.max(jnp.transpose(rows_ref[b, :]), axis=0, keepdims=True)
        from_half = jnp.max(columns_ref[:, b], axis=0, keepdims=True)
        low, high = (from_half, nothing) if g < groups else (nothing, from_half)
        mine = jnp.maximum(own_ref[:1, a], jnp.where(core == 0, from_all, high))
        theirs = jnp.where(core == 0, low, from_all)
        out_ref[g * 8 : (g + 1) * 8, :] = jnp.where(
            parity == core, jnp.broadcast_to(mine, (8, LANES)), jnp.broadcast_to(theirs, (8, LANES))
        )


def cross_pairs(x, y, z, own, width):
    half = y.shape[0] * CAP
    cost = pl.CostEstimate(flops=2 * half * half * width, bytes_accessed=4 * half * width, transcendentals=0)
    vmem = pl.BlockSpec(memory_space=pltpu.VMEM)
    scratch = [
        pltpu.VMEM((half, LANES), jnp.float32),
        pltpu.VMEM((8, half), jnp.float32),
        pltpu.VMEM((half, LANES), jnp.float32),
    ]
    params = pltpu.CompilerParams(vmem_limit_bytes=24 * 2**20)
    first, columns = pl.pallas_call(
        first_kernel,
        out_shape=(jax.ShapeDtypeStruct((8, half), jnp.float32),) * 2,
        in_specs=[vmem] * 2,
        out_specs=(vmem,) * 2,
        scratch_shapes=scratch,
        compiler_params=params,
        cost_estimate=cost,
        name="cross_first",
    )(x, y)
    return pl.pallas_call(
        second_kernel,
        out_shape=jax.ShapeDtypeStruct((2 * half // LANES * 8, LANES), jnp.float32),
        in_specs=[vmem] * 6,
        out_specs=vmem,
        scratch_shapes=scratch + [pltpu.VMEM((8, half), jnp.float32)],
        compiler_params=params,
        cost_estimate=cost,
        name="cross_second",
    )(x, y, z, own, first, columns)


def pick_kernel(recv_ref, target_ref, out_ref):
    pairs = recv_ref.shape[0]
    owners = pairs // 2
    best = jnp.maximum(
        recv_ref[pl.ds(0, owners, stride=2), :], recv_ref[pl.ds(1, owners, stride=2), :]
    )
    target = target_ref[...]
    rows = target.shape[1]
    cid = target >> 5
    slot = (target & (CAP - 1)) + lax.axis_index("owner") % PER_ROW * CAP
    chosen = lax.broadcasted_iota(jnp.int32, (owners, rows), 0) == cid
    chosen = chosen.astype(jnp.float32).astype(jnp.bfloat16)
    total = jnp.zeros((LANES, rows), jnp.float32)
    rest = best
    for _ in range(3):
        piece = rest.astype(jnp.bfloat16)
        rest = rest - piece.astype(jnp.float32)
        total += lax.dot_general(
            piece, chosen, (((0,), (0,)), ((), ())), preferred_element_type=jnp.float32
        )
    mine = lax.broadcasted_iota(jnp.int32, (LANES, rows), 0) == slot
    out_ref[...] = jnp.sum(jnp.where(mine, total, 0.0), axis=0, keepdims=True)


def pick(recv, target):
    return pl.pallas_call(
        pick_kernel,
        out_shape=jax.ShapeDtypeStruct(target.shape, jnp.float32),
        in_specs=[pl.BlockSpec(memory_space=pltpu.VMEM)] * 2,
        out_specs=pl.BlockSpec(memory_space=pltpu.VMEM),
        compiler_params=pltpu.CompilerParams(vmem_limit_bytes=8 * 2**20),
        name="pick_results",
    )(recv, target)


def shards(embeddings, cluster, order):
    owners = lax.axis_size("owner")
    rows, width = embeddings.shape
    cid, rank = lax.optimization_barrier((cluster.reshape(1, rows), order.reshape(1, rows)))
    code = cid * 65536 + rank
    packed, target = pack(embeddings, code, owners)
    mine = lax.all_to_all(packed, "owner", split_axis=0, concat_axis=0, tiled=True)
    swap = [(0, 1), (1, 0)]
    half = owners // 2
    first = lax.ppermute(mine[:half], "split", swap)
    second = lax.ppermute(mine[half:], "split", swap)
    own = own_pairs(mine, width)
    best = cross_pairs(mine, first, second, own, width)
    returned = lax.all_to_all(best, ("owner", "split"), split_axis=0, concat_axis=0, tiled=True)
    return pick(returned, target).reshape(rows)


def solution(mesh):
    return jax.shard_map(
        shards,
        mesh=mesh,
        in_specs=(P(("owner", "split"), None), P(("owner", "split"), None), P(("owner", "split"))),
        out_specs=P(("owner", "split")),
        check_vma=False,
    )
```
